256 devices in a mesh: row: 16 (over z, core), col: 16 (over x, y).
Axes of the slice: x: 4, y: 4, z: 8, core: 2. Of those that a mesh axis runs over, the one named last changes fastest.
Arguments:
- context: bfloat16 [4096, 6144], P('row', 'col'), may hold values from -6 to 6
- residual_in: bfloat16 [4096, 6144], P('col', 'row'), may hold values from -70 to 70
- proj_weight: bfloat16 [6144, 6144], P('col', 'row'), may hold values from -0.078125 to 0.078125
- proj_bias: bfloat16 [6144], P('row'), may hold values from -3 to 3
- norm_gain: bfloat16 [6144], P('row'), may hold values from 0.099609375 to 1.8984375
- norm_shift: bfloat16 [6144], P('row'), may hold values from -3 to 3
- up_weight: bfloat16 [6144, 12288], P('row', 'col'), may hold values from -0.078125 to 0.078125
- up_bias: bfloat16 [12288], P('col'), may hold values from -3 to 3
- down_weight: bfloat16 [12288, 6144], P('col', 'row'), may hold values from -0.0546875 to 0.0546875
- down_bias: bfloat16 [6144], P('row'), may hold values from -3 to 3
Outputs:
- layer_out: bfloat16 [4096, 6144], P('col', 'row')
The draws below stay inside these ranges and needn't reach their ends.
All inputs are finite; a program needn't handle non-finite values.
Results may differ from the reference program's by a relative error of at most 0.015.
Values may be sent and summed in bfloat16 or wider, within the bound.
A program may use at most 64 MiB of HBM per device.

```python
import jax
import jax.numpy as jnp
from jax import lax

D = 6144
FF = 12288
TOKENS = 4096
N_ROW = 16
N_COL = 16


def draw_residual_in(key, part):
    key = jax.random.fold_in(key, 7)
    base_key, col_key, row_key = jax.random.split(key, 3)
    position = jnp.arange(D, dtype=jnp.float32) / D
    col_scale = 0.3 * jnp.power(10.0, position) * jnp.exp(jax.random.uniform(col_key, (D,), jnp.float32, -0.2, 0.2))
    row_scale = jnp.exp(jax.random.uniform(row_key, (TOKENS, 1), jnp.float32, jnp.log(0.3), jnp.log(3.0)))
    base = jnp.clip(jax.random.normal(base_key, (TOKENS, D), jnp.float32), -6.0, 6.0)
    return (base * row_scale * col_scale).astype(jnp.bfloat16)


def steps_of(key, shape, cuts, smallest, largest):
    gain, own = 1.0, jax.random.fold_in(key, 6)
    for axis_at, blocks in cuts:
        steps = jnp.exp(jax.random.uniform(jax.random.fold_in(own, axis_at), (blocks,), jnp.float32, smallest / len(cuts), largest / len(cuts)))
        gain = gain * jnp.repeat(steps, shape[axis_at] // blocks).reshape([-1 if axis == axis_at else 1 for axis in range(len(shape))])
    return gain


def centred(key, shape, spread, reach, shards=(), kind=jnp.bfloat16):
    array = spread * jax.random.normal(key, shape, jnp.float32)
    if shards:
        array = array * steps_of(key, shape, shards, -0.22, 0.18)
    return jnp.clip(array, -reach, reach).astype(kind)


def setup_inputs(seed: int = 0) -> dict:
    splits = jax.random.split(jax.random.key(seed), 11)
    context = centred(splits[0], (TOKENS, D), 1.0, 6.0, ((0, 16), (1, 16)))
    residual_in = draw_residual_in(jax.random.fold_in(splits[10], 71), 0)
    proj_weight = centred(splits[2], (D, D), D ** -0.5, 0.078125, ((0, 16), (1, 16)))
    proj_bias = centred(splits[3], (D,), 0.5, 3.0, ((0, 16),))
    norm_gain = jnp.clip(1.0 + 0.18 * jax.random.normal(splits[4], (D,), jnp.float32), 0.099609375, 1.8984375).astype(jnp.bfloat16)
    norm_shift = centred(splits[5], (D,), 0.5, 3.0, ((0, 16),))
    up_weight = centred(splits[6], (D, FF), D ** -0.5, 0.078125, ((0, 16), (1, 16)))
    up_bias = centred(splits[7], (FF,), 0.5, 3.0, ((0, 16),))
    down_weight = centred(splits[8], (FF, D), FF ** -0.5, 0.0546875, ((0, 16), (1, 16)))
    down_bias = centred(splits[9], (D,), 0.5, 3.0, ((0, 16),))
    return {"context": context, "residual_in": residual_in, "proj_weight": proj_weight, "proj_bias": proj_bias, "norm_gain": norm_gain, "norm_shift": norm_shift, "up_weight": up_weight, "up_bias": up_bias, "down_weight": down_weight, "down_bias": down_bias}


def block_sum(left, right, parts):
    width = left.shape[1] // parts

    def add_block(index, total):
        start = index * width
        left_part = lax.dynamic_slice_in_dim(left, start, width, 1)
        right_part = lax.dynamic_slice_in_dim(right, start, width, 0)
        term = jnp.dot(left_part, right_part, preferred_element_type=jnp.float32)
        return total + term.astype(jnp.bfloat16).astype(jnp.float32)
    empty = jnp.zeros((left.shape[0], right.shape[1]), jnp.float32)
    return lax.fori_loop(0, parts, add_block, empty)

def reference(context, residual_in, proj_weight, proj_bias, norm_gain, norm_shift, up_weight, up_bias, down_weight, down_bias):
    attended = block_sum(context, proj_weight, N_COL)
    mixed = residual_in.astype(jnp.float32) + attended + proj_bias.astype(jnp.float32)
    mean = lax.optimization_barrier(jnp.sum(mixed, axis=1, keepdims=True)) / D
    var = lax.optimization_barrier(jnp.sum(mixed * mixed, axis=1, keepdims=True)) / D - mean * mean
    normed = ((mixed - mean) * lax.rsqrt(var + 1e-05) * norm_gain.astype(jnp.float32) + norm_shift.astype(jnp.float32)).astype(jnp.bfloat16)
    pre = block_sum(normed, up_weight, N_ROW) + up_bias.astype(jnp.float32)
    hidden = jax.nn.gelu(pre, approximate=True).astype(jnp.bfloat16)
    result = mixed + block_sum(hidden, down_weight, N_COL) + down_bias.astype(jnp.float32)
    return result.astype(jnp.bfloat16)
```

```python
import functools

import jax
import jax.numpy as jnp
from jax import lax
from jax.experimental import pallas as pl
from jax.experimental.pallas import tpu as pltpu
from jax.sharding import PartitionSpec as P

D = 6144
F = 384
S = 4
T = 128 // S
NZ, NX, NY = 8, 4, 4
MESH = pl.DeviceIdType.MESH
STARTS = (
    ("spread", 0.0, 1.0),
    ("project", 6.0, 12.0),
    ("reduce_mid", 10.0, 12.0),
    ("mix", 14.0, 12.0),
    ("norm", 18.0, 12.0),
    ("forward", 22.0, 12.0),
    ("up", 26.0, 12.0),
    ("gelu", 36.0, 12.0),
    ("down", 46.0, 12.0),
    ("reduce_out", 51.0, 12.0),
    ("finish", 56.0, 12.0),
)
SLOTS = {"spread": 0, "project": 7, "reduce_mid": 13, "mix": 19, "norm": 26, "forward": 32, "up": 38, "gelu": 45,
         "down": 52, "reduce_out": 58, "finish": 64, "swap": 65}
N_SLOTS = 66


def kernel(ctx, res, wp, pb, ng, ns, wu, ub, wd, db, out,
           ctx_all, wproj, wup, wdown, resb, vec, att, rs1, red, rs2, mixed, st, nrm, prep, zr, hid,
           outp, os1, ored, os2, obuf, ssem, rsem, wssem, wrsem, lsem):
    r, q = lax.axis_index("row"), lax.axis_index("col")
    z, c = r // 2, r % 2
    x, y = q // 4, q % 4
    sib = (z * 2 + 1 - c, q)

    def zi(d):
        return (z + d) % NZ

    def xi(d):
        return (x + d) % NX

    def yi(d):
        return (y + d) % NY

    def zp(d):
        return (zi(d) * 2 + c, q)

    def xp(d):
        return (r, xi(d) * 4 + y)

    def yp(d):
        return (r, x * 4 + yi(d))

    barrier = pltpu.get_barrier_semaphore()
    partners = [sib] + [zp(d) for d in range(1, NZ)] + [xp(d) for d in range(1, NX)] + [yp(d) for d in range(1, NY)]
    for p in partners:
        pl.semaphore_signal(barrier, inc=1, device_id=p, device_id_type=MESH)
    pl.semaphore_wait(barrier, len(partners))

    started = []

    def remote(src, dst, send, recv, device):
        copy = pltpu.make_async_remote_copy(
            src_ref=src, dst_ref=dst, send_sem=send, recv_sem=recv, device_id=device, device_id_type=MESH
        )
        copy.start()
        started.append(copy)
        return copy

    def local(src, dst, sem):
        copy = pltpu.make_async_copy(src, dst, sem)
        copy.start()
        return copy

    def rows(start, size):
        return pl.ds(pl.multiple_of(start, 16), size)

    mine = pl.ds(pl.multiple_of(c * F, 128), F)
    my_rows = rows(c * F, F)
    ctx_in = {}
    for s in range(S):
        ctx_in[s] = (
            remote(ctx.at[rows((1 - c) * 128 + s * T, T)], ctx_all.at[s, z, c],
                   ssem.at[s, SLOTS["swap"]], rsem.at[s, SLOTS["swap"]], sib),
            local(ctx.at[rows(c * 128 + s * T, T)], ctx_all.at[s, z, c], lsem.at[s]),
        )
    vec[c, 0:1, :] = pb[...].astype(jnp.float32)
    vec[c, 1:2, :] = ng[...].astype(jnp.float32)
    vec[c, 2:3, :] = ns[...].astype(jnp.float32)
    vec[c, 3:4, :] = db[...].astype(jnp.float32)
    w_in = {
        "proj": (remote(wp, wproj.at[:, mine], wssem.at[0], wrsem.at[0], sib), local(wp, wproj.at[:, mine], lsem.at[S])),
        "res": (
            remote(res.at[rows((1 - c) * 128, 128)], resb.at[c], wssem.at[1], wrsem.at[1], sib),
            local(res.at[rows(c * 128, 128)], resb.at[c], lsem.at[S + 1]),
        ),
        "vec": (remote(vec.at[c], vec.at[c], wssem.at[2], wrsem.at[2], sib),),
        "up": (remote(wu, wup.at[my_rows], wssem.at[3], wrsem.at[3], sib), local(wu, wup.at[my_rows], lsem.at[S + 2])),
        "down": (remote(wd, wdown.at[:, mine], wssem.at[4], wrsem.at[4], sib), local(wd, wdown.at[:, mine], lsem.at[S + 3])),
    }

    def ready(name):
        if name in w_in:
            copies = w_in.pop(name)
            copies[0].wait_recv()
            for copy in copies[1:]:
                copy.wait()

    flights = {}

    def send(name, s, moves):
        base = SLOTS[name]
        flights[name, s] = [
            remote(src, dst, ssem.at[s, base + i], rsem.at[s, base + i], device)
            for i, (src, dst, device) in enumerate(moves)
        ]

    def arrive(name, s):
        for copy in flights[name, s]:
            copy.wait_recv()

    def spread(s):
        ctx_in[s][0].wait_recv()
        ctx_in[s][1].wait()
        send("spread", s, [(ctx_all.at[s, z], ctx_all.at[s, z], zp(d)) for d in range(1, NZ)])

    def scatter_first(name, s, product, part, landing):
        product = product.astype(jnp.bfloat16)
        part[s, 0] = product[:, :F].reshape(NX, NY, T, F)
        for i in range(NX):
            for j in range(NY):
                part[s, 1, j, i] = product[(i * NY + j) * T:(i * NY + j + 1) * T, F:]
        send(name, s, [(part.at[s, 0, xi(d)], landing.at[s, 0, d - 1], xp(d)) for d in range(1, NX)]
             + [(part.at[s, 1, yi(d)], landing.at[s, 1, d - 1], yp(d)) for d in range(1, NY)])

    def scatter_second(source, name, s, part, landing, reduced, landing2):
        arrive(source, s)
        for h, own in ((0, x), (1, y)):
            total = part[s, h, own].astype(jnp.float32)
            for d in range(3):
                total = total + landing[s, h, d].astype(jnp.float32)
            reduced[s, h] = total.astype(jnp.bfloat16)
        send(name, s, [(reduced.at[s, 0, yi(d)], landing2.at[s, 0, d - 1], yp(d)) for d in range(1, NY)]
             + [(reduced.at[s, 1, xi(d)], landing2.at[s, 1, d - 1], xp(d)) for d in range(1, NX)])

    def scattered(source, s, reduced, landing2):
        arrive(source, s)
        totals = []
        for h, own in ((0, y), (1, x)):
            total = reduced[s, h, own].astype(jnp.float32)
            for d in range(3):
                total = total + landing2[s, h, d].astype(jnp.float32)
            totals.append(total)
        return totals

    def project(s):
        arrive("spread", s)
        ready("proj")
        product = jnp.dot(ctx_all[s].reshape(16 * T, F), wproj[...], preferred_element_type=jnp.float32)
        scatter_first("project", s, product, att, rs1)

    def reduce_mid(s):
        scatter_second("project", "reduce_mid", s, att, rs1, red, rs2)

    def mix(s):
        totals = scattered("reduce_mid", s, red, rs2)
        ready("res")
        ready("vec")
        row_sum, row_square = 0.0, 0.0
        for h in range(2):
            value = resb[h, s * T:(s + 1) * T, :].astype(jnp.float32) + totals[h] + vec[h, 0:1, :]
            mixed[s, h] = value
            row_sum = row_sum + jnp.sum(value, axis=1, keepdims=True)
            row_square = row_square + jnp.sum(value * value, axis=1, keepdims=True)
        lane = lax.broadcasted_iota(jnp.int32, (T, 128), 1)
        st[s, z] = jnp.where(lane < 64, row_sum, row_square)
        send("mix", s, [(st.at[s, z], st.at[s, z], zp(d)) for d in range(1, NZ)])

    def norm(s):
        arrive("mix", s)
        total = jnp.sum(st[s], axis=0)
        mean = total[:, 0:1] / D
        var = total[:, 64:65] / D - mean * mean
        scale = lax.rsqrt(var + 1e-05)
        for h in range(2):
            normed = (mixed[s, h] - mean) * scale * vec[h, 1:2, :] + vec[h, 2:3, :]
            nrm[s, x, y, :, h * F:(h + 1) * F] = normed.astype(jnp.bfloat16)
        left, right = nrm.at[s, x, y, :, 0:F], nrm.at[s, x, y, :, F:2 * F]
        send("norm", s, [(left, left, xp(d)) for d in range(1, NX)] + [(right, right, yp(d)) for d in range(1, NY)])

    def forward(s):
        arrive("norm", s)
        left, right = nrm.at[s, :, y, :, 0:F], nrm.at[s, x, :, :, F:2 * F]
        send("forward", s, [(left, left, yp(d)) for d in range(1, NY)] + [(right, right, xp(d)) for d in range(1, NX)])

    def up(s):
        arrive("forward", s)
        ready("up")
        product = jnp.dot(nrm[s].reshape(16 * T, 2 * F), wup[...], preferred_element_type=jnp.float32)
        prep[s] = product.astype(jnp.bfloat16).reshape(NZ, 2 * T, 2 * F)
        send("up", s, [(prep.at[s, zi(d)], zr.at[s, d - 1], zp(d)) for d in range(1, NZ)])

    def gelu(s):
        arrive("up", s)
        total = prep[s, z].astype(jnp.float32) + ub[...].astype(jnp.float32)
        for d in range(7):
            total = total + zr[s, d].astype(jnp.float32)
        hid[s, z] = jax.nn.gelu(total, approximate=True).astype(jnp.bfloat16)
        send("gelu", s, [(hid.at[s, z], hid.at[s, z], zp(d)) for d in range(1, NZ)])

    def down(s):
        arrive("gelu", s)
        ready("down")
        product = jnp.dot(hid[s].reshape(16 * T, 2 * F), wdown[...], preferred_element_type=jnp.float32)
        scatter_first("down", s, product, outp, os1)

    def reduce_out(s):
        scatter_second("down", "reduce_out", s, outp, os1, ored, os2)

    out_local = []

    def finish(s):
        totals = scattered("reduce_out", s, ored, os2)
        for h in range(2):
            obuf[s, h] = (mixed[s, h] + totals[h] + vec[h, 3:4, :]).astype(jnp.bfloat16)
        place = out.at[rows(c * 128 + s * T, T)]
        send("finish", s, [(obuf.at[s, 1 - c], place, sib)])
        out_local.append(local(obuf.at[s, c], place, lsem.at[s]))

    stages = dict(spread=spread, project=project, reduce_mid=reduce_mid, mix=mix, norm=norm, forward=forward,
                  up=up, gelu=gelu, down=down, reduce_out=reduce_out, finish=finish)
    order = sorted((start + s * gap, place, s, name) for place, (name, start, gap) in enumerate(STARTS) for s in range(S))
    for _, _, s, name in order:
        stages[name](s)
    for s in range(S):
        arrive("finish", s)
    for copy in out_local:
        copy.wait()
    for copy in started:
        copy.wait_send()


def local_step(context, residual_in, proj_weight, proj_bias, norm_gain, norm_shift, up_weight, up_bias, down_weight, down_bias):
    bf16, f32 = jnp.bfloat16, jnp.float32
    vmem, hbm = pl.BlockSpec(memory_space=pltpu.VMEM), pl.BlockSpec(memory_space=pl.ANY)
    return pl.pallas_call(
        kernel,
        out_shape=jax.ShapeDtypeStruct((256, F), bf16),
        in_specs=[hbm, hbm, hbm, vmem, vmem, vmem, hbm, vmem, hbm, vmem],
        out_specs=hbm,
        scratch_shapes=[
            pltpu.VMEM((S, NZ, 2, T, F), bf16),
            pltpu.VMEM((F, 2 * F), bf16),
            pltpu.VMEM((2 * F, 2 * F), bf16),
            pltpu.VMEM((2 * F, 2 * F), bf16),
            pltpu.VMEM((2, 128, F), bf16),
            pltpu.VMEM((2, 8, F), f32),
            pltpu.VMEM((S, 2, 4, 4, T, F), bf16),
            pltpu.VMEM((S, 2, 3, 4, T, F), bf16),
            pltpu.VMEM((S, 2, 4, T, F), bf16),
            pltpu.VMEM((S, 2, 3, T, F), bf16),
            pltpu.VMEM((S, 2, T, F), f32),
            pltpu.VMEM((S, NZ, T, 128), f32),
            pltpu.VMEM((S, NX, NY, T, 2 * F), bf16),
            pltpu.VMEM((S, NZ, 2 * T, 2 * F), bf16),
            pltpu.VMEM((S, NZ - 1, 2 * T, 2 * F), bf16),
            pltpu.VMEM((S, NZ, 2 * T, 2 * F), bf16),
            pltpu.VMEM((S, 2, 4, 4, T, F), bf16),
            pltpu.VMEM((S, 2, 3, 4, T, F), bf16),
            pltpu.VMEM((S, 2, 4, T, F), bf16),
            pltpu.VMEM((S, 2, 3, T, F), bf16),
            pltpu.VMEM((S, 2, T, F), bf16),
            pltpu.SemaphoreType.DMA((S, N_SLOTS)),
            pltpu.SemaphoreType.DMA((S, N_SLOTS)),
            pltpu.SemaphoreType.DMA((5,)),
            pltpu.SemaphoreType.DMA((5,)),
            pltpu.SemaphoreType.DMA((S + 4,)),
        ],
        compiler_params=pltpu.CompilerParams(
            collective_id=0, has_side_effects=True, vmem_limit_bytes=56 * 2**20
        ),
        name="layer",
    )(context, residual_in, proj_weight, proj_bias.reshape(1, F), norm_gain.reshape(1, F), norm_shift.reshape(1, F),
      up_weight, up_bias.reshape(1, 2 * F), down_weight, down_bias.reshape(1, F))


def solution(mesh):
    return jax.shard_map(
        local_step,
        mesh=mesh,
        in_specs=(
            P("row", "col"),
            P("col", "row"),
            P("col", "row"),
            P("row"),
            P("row"),
            P("row"),
            P("row", "col"),
            P("col"),
            P("col", "row"),
            P("row"),
        ),
        out_specs=P("col", "row"),
        check_vma=False,
    )
```

```python
import jax
import jax.numpy as jnp
from jax import lax
from jax.experimental import pallas as pl
from jax.experimental.pallas import tpu as pltpu
from jax.sharding import PartitionSpec as P

D = 6144
F = 384
H = 128
CHUNKS = (32, 32, 32, 32)
GROUPS = ((1,), (2, 3))
S = len(CHUNKS)
OFFSETS = tuple(sum(CHUNKS[:s]) for s in range(S))
NZ, NX, NY = 8, 4, 4
MESH = pl.DeviceIdType.MESH

RING = tuple((2, "z", 3072 * part, 2.2) for part in (1, 1, 1, 0.5))
CHAIN = (
    ("project", 6, "xy", 6144, 2.8, 0.016),
    ("reduce_mid", 6, "xy", 1536, 2.8, 0.01),
    ("mix", 7, "z", 0, 4.0, 0.01),
    ("norm", 6, "xy", 1536, 2.8, 0.01),
    ("forward", 6, "xy", 6144, 2.8, 0.0),
    ("up", 2, "z", 1536, 2.2, 0.024),
    ("pass1", 2, "z", 3072, 2.2, 0.008),
    ("pass2", 2, "z", 3072, 2.2, 0.008),
    ("pass3", 2, "z", 3072, 2.2, 0.008),
    ("gelu", 2, "z", 3072, 2.2, 0.016),
    ("hand1", 2, "z", 3072, 2.2, 0.0),
    ("hand2", 2, "z", 3072, 2.2, 0.0),
    ("hand3", 2, "z", 1536, 2.2, 0.0),
    ("down", 6, "xy", 6144, 2.8, 0.024),
    ("reduce_out", 6, "xy", 1536, 2.8, 0.01),
    ("finish", 1, "core", 0, 1.0, 0.01),
)
RATE = 65000.0


def issue_order():
    ring = tuple(("ctx%d" % t, 2, "z", 1536 * (0.5 if t == 3 else 1), 2.2, 0.0) for t in range(4))
    chains = [[("spread", 7, "z", 12288, 4.0, 0.0, 0, CHUNKS[0])] + [st + (0, CHUNKS[0]) for st in CHAIN]]
    chains += [[st + (s, CHUNKS[s]) for st in CHAIN] for s in range(1, S)]
    for g, members in enumerate(GROUPS):
        chains.append([st + (g, sum(CHUNKS[s] for s in members)) for st in ring])
    waits = {s: S + g for g, members in enumerate(GROUPS) for s in members}
    place, ready = [0] * len(chains), [0.0] * len(chains)
    for s in range(1, S):
        ready[s] = float("inf")
    free, now, order = {"z": 0.0, "xy": 0.0, "core": 0.0}, 0.0, []
    while any(p < len(ch) for p, ch in zip(place, chains)):
        live = [i for i in range(len(chains)) if place[i] < len(chains[i])]
        first = min(ready[i] for i in live)
        due = [i for i in live if ready[i] <= max(now, first)]
        i = min(due)
        name, copies, link, size, latency, work, index, tokens = chains[i][place[i]]
        now = max(now, ready[i]) + work * tokens + 0.06 * copies
        free[link] = max(free[link], now) + size * tokens / RATE
        ready[i] = free[link] + latency
        place[i] += 1
        order.append((name, index))
        if i >= S and place[i] == len(chains[i]):
            for s, chain in waits.items():
                if chain == i:
                    ready[s] = ready[i]
    return order, max(ready[:S])


def kernel(ctx, res, wp, pb, ng, ns, wu, ub, wd, db, out,
           ctx_all, wproj, wup, wdown, resb, vin0, vin1, vin2, vin3, uin, vec, att, rs1, red, rs2, mixed, st, nrm, prep, zr, hid,
           outp, os1, ored, os2, obuf, ssem, rsem, wssem, wrsem, lsem):
    r, q = lax.axis_index("row"), lax.axis_index("col")
    z, c = r // 2, r % 2
    x, y = q // 4, q % 4
    sib = (z * 2 + 1 - c, q)

    def zi(d):
        return (z + d + NZ) % NZ

    def xi(d):
        return (x + d) % NX

    def yi(d):
        return (y + d) % NY

    def zp(d):
        return (zi(d) * 2 + c, q)

    def xp(d):
        return (r, xi(d) * 4 + y)

    def yp(d):
        return (r, x * 4 + yi(d))

    def rows(start, size):
        return pl.ds(pl.multiple_of(start, 16), size)

    def local(src, dst, sem):
        copy = pltpu.make_async_copy(src, dst, sem)
        copy.start()
        return copy

    sends = []

    def remote(src, dst, send, recv, device):
        copy = pltpu.make_async_remote_copy(
            src_ref=src, dst_ref=dst, send_sem=send, recv_sem=recv, device_id=device, device_id_type=MESH
        )
        copy.start()
        sends.append(copy)
        return copy

    vin = (vin0, vin1, vin2, vin3)
    mine = pl.ds(pl.multiple_of(c * F, 128), F)
    my_rows = rows(c * F, F)
    near, far = c * H, (1 - c) * H
    early = CHUNKS[0]
    own = {
        "first": [local(ctx.at[rows(near, early)], ctx_all.at[z, c, 0:early], lsem.at[0])],
        "vec": [local(v, vin[i], lsem.at[1 + i]) for i, v in enumerate((pb, ng, ns, db))],
        "rest": [local(ctx.at[rows(near + early, H - early)], ctx_all.at[z, c, early:H], lsem.at[5])],
        "proj": [local(wp, wproj.at[:, mine], lsem.at[6])],
        "res": [local(res.at[rows(near, H)], resb.at[c], lsem.at[7])],
        "up": [local(wu, wup.at[my_rows], lsem.at[8]), local(ub, uin, lsem.at[9])],
        "down": [local(wd, wdown.at[:, mine], lsem.at[10])],
    }
    barrier = pltpu.get_barrier_semaphore()
    partners = [sib] + [zp(d) for d in range(1, NZ)] + [xp(d) for d in range(1, NX)] + [yp(d) for d in range(1, NY)]
    for p in partners:
        pl.semaphore_signal(barrier, inc=1, device_id=p, device_id_type=MESH)
    pl.semaphore_wait(barrier, len(partners))

    def swap(i, src, dst):
        return remote(src, dst, wssem.at[i], wrsem.at[i], sib)

    theirs = {
        "first": swap(0, ctx.at[rows(far, early)], ctx_all.at[z, c, 0:early]),
        "rest": swap(1, ctx.at[rows(far + early, H - early)], ctx_all.at[z, c, early:H]),
        "proj": swap(2, wp, wproj.at[:, mine]),
        "res": swap(3, res.at[rows(far, H)], resb.at[c]),
    }
    for copy in own.pop("vec"):
        copy.wait()
    for i in range(4):
        vec[c, i:i + 1, :] = vin[i][...].reshape(1, F).astype(jnp.float32)
    theirs["vec"] = swap(4, vec.at[c], vec.at[c])
    theirs["up"] = swap(5, wu, wup.at[my_rows])
    theirs["down"] = swap(6, wd, wdown.at[:, mine])

    def ready(name):
        if name in theirs:
            theirs.pop(name).wait_recv()
            for copy in own.pop(name, ()):
                copy.wait()

    flights, slots = {}, {}

    def send(name, s, moves):
        copies = []
        for src, dst, device in moves:
            i = slots[s] = slots.get(s, -1) + 1
            copies.append(remote(src, dst, ssem.at[s, i], rsem.at[s, i], device))
        flights[name, s] = copies

    def arrive(name, s):
        for copy in flights[name, s]:
            copy.wait_recv()

    def clear(keep):
        while len(sends) > keep:
            sends.pop(0).wait_send()

    def part(s):
        return slice(OFFSETS[s], OFFSETS[s] + CHUNKS[s])

    def spread(s):
        ready("first")
        piece = ctx_all.at[z, :, part(0), :]
        send("spread", 0, [(piece, piece, zp(d)) for d in (4, 3, 5, 2, 6, 1, 7)])

    def ring(t):
        def step(g):
            members = GROUPS[g]
            span = slice(OFFSETS[members[0]], OFFSETS[members[-1]] + CHUNKS[members[-1]])
            if t == 0:
                ready("rest")
            else:
                arrive("ctx%d" % (t - 1), S + g)
            blocks = (0, 1) if t == 3 else (slice(0, 2), slice(0, 2))
            up_piece, down_piece = ctx_all.at[zi(-t), blocks[0], span, :], ctx_all.at[zi(t), blocks[1], span, :]
            send("ctx%d" % t, S + g, [(up_piece, up_piece, zp(1)), (down_piece, down_piece, zp(-1))])
        return step

    def scatter_first(name, s, product, piece, landing):
        product, k, t = product.astype(jnp.bfloat16), part(s), CHUNKS[s]
        piece[0, :, :, k, :] = product[:, :F].reshape(NX, NY, t, F)
        for i in range(NX):
            for j in range(NY):
                piece[1, j, i, k, :] = product[(i * NY + j) * t:(i * NY + j + 1) * t, F:]
        send(name, s, [
            move
            for d in (1, 3, 2)
            for move in (
                (piece.at[0, xi(d), :, k, :], landing.at[0, d - 1, :, k, :], xp(d)),
                (piece.at[1, yi(d), :, k, :], landing.at[1, d - 1, :, k, :], yp(d)),
            )
        ])

    def scatter_second(source, name, s, piece, landing, reduced, landing2):
        arrive(source, s)
        k = part(s)
        for h, own_at in ((0, x), (1, y)):
            total = piece[h, own_at, :, k, :].astype(jnp.float32)
            for d in range(3):
                total = total + landing[h, d, :, k, :].astype(jnp.float32)
            reduced[h, :, k, :] = total.astype(jnp.bfloat16)
        send(name, s, [
            move
            for d in (1, 3, 2)
            for move in (
                (reduced.at[0, yi(d), k, :], landing2.at[0, d - 1, k, :], yp(d)),
                (reduced.at[1, xi(d), k, :], landing2.at[1, d - 1, k, :], xp(d)),
            )
        ])

    def scattered(source, s, reduced, landing2):
        arrive(source, s)
        k, totals = part(s), []
        for h, own_at in ((0, y), (1, x)):
            total = reduced[h, own_at, k, :].astype(jnp.float32)
            for d in range(3):
                total = total + landing2[h, d, k, :].astype(jnp.float32)
            totals.append(total)
        return totals

    def project(s):
        if s == 0:
            arrive("spread", 0)
        else:
            g = [s in members for members in GROUPS].index(True)
            if ("ctx3", S + g) in flights:
                arrive("ctx3", S + g)
                del flights["ctx3", S + g]
        ready("proj")
        product = jnp.dot(ctx_all[:, :, part(s), :].reshape(16 * CHUNKS[s], F), wproj[...], preferred_element_type=jnp.float32)
        scatter_first("project", s, product, att, rs1)

    def reduce_mid(s):
        scatter_second("project", "reduce_mid", s, att, rs1, red, rs2)

    def mix(s):
        totals = scattered("reduce_mid", s, red, rs2)
        ready("res")
        ready("vec")
        k, t = part(s), CHUNKS[s]
        row_sum, row_square = jnp.zeros((t, 128), jnp.float32), jnp.zeros((t, 128), jnp.float32)
        for h in range(2):
            value = resb[h, k, :].astype(jnp.float32) + totals[h] + vec[h, 0:1, :]
            mixed[h, k, :] = value
            for i in range(0, F, 128):
                row_sum = row_sum + value[:, i:i + 128]
                row_square = row_square + value[:, i:i + 128] * value[:, i:i + 128]
        pad = jnp.zeros((64 - t, 128), jnp.float32)
        lanes = jnp.concatenate([row_sum, pad, row_square, pad], axis=0).T
        st[s, z] = jnp.sum(lanes, axis=0, keepdims=True)
        send("mix", s, [(st.at[s, z], st.at[s, z], zp(d)) for d in (4, 3, 5, 2, 6, 1, 7)])

    def norm(s):
        arrive("mix", s)
        k, t = part(s), CHUNKS[s]
        total = jnp.broadcast_to(jnp.sum(st[s], axis=0), (128, 128)).T
        mean = total[0:t, 0:1] / D
        var = total[64:64 + t, 0:1] / D - mean * mean
        scale = lax.rsqrt(var + 1e-05)
        for h in range(2):
            normed = (mixed[h, k, :] - mean) * scale * vec[h, 1:2, :] + vec[h, 2:3, :]
            nrm[x, y, k, h * F:(h + 1) * F] = normed.astype(jnp.bfloat16)
        left, right = nrm.at[x, y, k, 0:F], nrm.at[x, y, k, F:2 * F]
        send("norm", s, [move for d in (1, 3, 2) for move in ((left, left, xp(d)), (right, right, yp(d)))])

    def forward(s):
        arrive("norm", s)
        left, right = nrm.at[:, y, part(s), 0:F], nrm.at[x, :, part(s), F:2 * F]
        send("forward", s, [move for d in (1, 3, 2) for move in ((left, left, yp(d)), (right, right, xp(d)))])

    def up(s):
        arrive("forward", s)
        ready("up")
        k, t = part(s), CHUNKS[s]
        product = jnp.dot(nrm[:, :, k, :].reshape(16 * t, 2 * F), wup[...], preferred_element_type=jnp.float32)
        prep[:, :, k, :] = product.astype(jnp.bfloat16).reshape(NZ, 2, t, 2 * F)
        send("up", s, [
            (prep.at[zi(4), 0, k, :], zr.at[0, 0, 0, k, :], zp(1)),
            (prep.at[zi(4), 1, k, :], zr.at[1, 0, 1, k, :], zp(-1)),
        ])

    def add(at, step, way, blocks, k):
        prep[at, blocks, k, :] = (
            prep[at, blocks, k, :].astype(jnp.float32) + zr[way, step, blocks, k, :].astype(jnp.float32)
        ).astype(jnp.bfloat16)

    def passing(t):
        def step(s):
            arrive("up" if t == 1 else "pass%d" % (t - 1), s)
            k = part(s)
            moves = []
            for way, sign in ((0, 1), (1, -1)):
                at = zi(sign * (4 - t))
                add(at, t - 1, way, way if t == 1 else slice(0, 2), k)
                moves.append((prep.at[at, :, k, :], zr.at[way, t, :, k, :], zp(sign)))
            send("pass%d" % t, s, moves)
        return step

    def gelu(s):
        arrive("pass3", s)
        k = part(s)
        total = prep[z, :, k, :].astype(jnp.float32) + zr[0, 3, :, k, :].astype(jnp.float32)
        total = total + zr[1, 3, :, k, :].astype(jnp.float32) + uin[...].reshape(1, 2 * F).astype(jnp.float32)
        hid[z, :, k, :] = jax.nn.gelu(total, approximate=True).astype(jnp.bfloat16)
        piece = hid.at[z, :, k, :]
        send("gelu", s, [(piece, piece, zp(1)), (piece, piece, zp(-1))])

    def handing(t):
        def step(s):
            arrive("gelu" if t == 1 else "hand%d" % (t - 1), s)
            blocks = (0, 1) if t == 3 else (slice(0, 2), slice(0, 2))
            up_piece, down_piece = hid.at[zi(-t), blocks[0], part(s), :], hid.at[zi(t), blocks[1], part(s), :]
            send("hand%d" % t, s, [(up_piece, up_piece, zp(1)), (down_piece, down_piece, zp(-1))])
        return step

    def down(s):
        arrive("hand3", s)
        ready("down")
        product = jnp.dot(hid[:, :, part(s), :].reshape(16 * CHUNKS[s], 2 * F), wdown[...], preferred_element_type=jnp.float32)
        scatter_first("down", s, product, outp, os1)

    def reduce_out(s):
        scatter_second("down", "reduce_out", s, outp, os1, ored, os2)

    out_local = []

    def finish(s):
        totals = scattered("reduce_out", s, ored, os2)
        k = part(s)
        for h in range(2):
            obuf[h, k, :] = (mixed[h, k, :] + totals[h] + vec[h, 3:4, :]).astype(jnp.bfloat16)
        place = out.at[rows(near + OFFSETS[s], CHUNKS[s])]
        send("finish", s, [(obuf.at[1 - c, k, :], place, sib)])
        out_local.append(local(obuf.at[c, k, :], place, lsem.at[11 + s]))

    stages = dict(spread=spread, project=project, reduce_mid=reduce_mid, mix=mix, norm=norm, forward=forward,
                  up=up, gelu=gelu, down=down, reduce_out=reduce_out, finish=finish)
    for t in range(1, 4):
        stages["pass%d" % t], stages["hand%d" % t] = passing(t), handing(t)
    for t in range(4):
        stages["ctx%d" % t] = ring(t)
    for name, index in issue_order()[0]:
        stages[name](index)
        clear(48)
    for s in range(S):
        arrive("finish", s)
    for copy in out_local:
        copy.wait()
    clear(0)


def layer(context, residual_in, proj_weight, proj_bias, norm_gain, norm_shift, up_weight, up_bias, down_weight, down_bias):
    bf16, f32 = jnp.bfloat16, jnp.float32
    hbm = pl.BlockSpec(memory_space=pl.ANY)
    return pl.pallas_call(
        kernel,
        out_shape=jax.ShapeDtypeStruct((2 * H, F), bf16),
        in_specs=[hbm] * 10,
        out_specs=hbm,
        scratch_shapes=[
            pltpu.VMEM((NZ, 2, H, F), bf16),
            pltpu.VMEM((F, 2 * F), bf16),
            pltpu.VMEM((2 * F, 2 * F), bf16),
            pltpu.VMEM((2 * F, 2 * F), bf16),
            pltpu.VMEM((2, H, F), bf16),
            *[pltpu.VMEM((F,), bf16)] * 4,
            pltpu.VMEM((2 * F,), bf16),
            pltpu.VMEM((2, 8, F), f32),
            pltpu.VMEM((2, 4, 4, H, F), bf16),
            pltpu.VMEM((2, 3, 4, H, F), bf16),
            pltpu.VMEM((2, 4, H, F), bf16),
            pltpu.VMEM((2, 3, H, F), bf16),
            pltpu.VMEM((2, H, F), f32),
            pltpu.VMEM((S, NZ, 1, 128), f32),
            pltpu.VMEM((NX, NY, H, 2 * F), bf16),
            pltpu.VMEM((NZ, 2, H, 2 * F), bf16),
            pltpu.VMEM((2, 4, 2, H, 2 * F), bf16),
            pltpu.VMEM((NZ, 2, H, 2 * F), bf16),
            pltpu.VMEM((2, 4, 4, H, F), bf16),
            pltpu.VMEM((2, 3, 4, H, F), bf16),
            pltpu.VMEM((2, 4, H, F), bf16),
            pltpu.VMEM((2, 3, H, F), bf16),
            pltpu.VMEM((2, H, F), bf16),
            pltpu.SemaphoreType.DMA((S + len(GROUPS), 80)),
            pltpu.SemaphoreType.DMA((S + len(GROUPS), 80)),
            pltpu.SemaphoreType.DMA((7,)),
            pltpu.SemaphoreType.DMA((7,)),
            pltpu.SemaphoreType.DMA((11 + S,)),
        ],
        compiler_params=pltpu.CompilerParams(
            collective_id=0, has_side_effects=True, vmem_limit_bytes=56 * 2**20
        ),
        name="layer",
    )(context, residual_in, proj_weight, proj_bias, norm_gain, norm_shift, up_weight, up_bias, down_weight, down_bias)


def solution(mesh):
    return jax.shard_map(
        layer,
        mesh=mesh,
        in_specs=(
            P("row", "col"),
            P("col", "row"),
            P("col", "row"),
            P("row"),
            P("row"),
            P("row"),
            P("row", "col"),
            P("col"),
            P("col", "row"),
            P("row"),
        ),
        out_specs=P("col", "row"),
        check_vma=False,
    )
```

```python
import jax
import jax.numpy as jnp
from jax import lax
from jax.experimental import pallas as pl
from jax.experimental.pallas import tpu as pltpu
from jax.sharding import PartitionSpec as P

D = 6144
F = 384
K = 4 * F
U = 8 * F
H = 64
S = 4
T = H // S
GROUPS = ((1,), (2, 3))
NZ, NX, NY = 8, 4, 4
MESH = pl.DeviceIdType.MESH

CHAIN = (
    ("project", 3, "y", 98304, 2.7, 0.6),
    ("mix", 7, "z", 0, 4.3, 0.6),
    ("norm", 3, "y", 98304, 2.7, 0.5),
    ("up", 2, "z", 49152, 2.8, 0.9),
    ("pass1", 2, "z", 98304, 2.8, 0.25),
    ("pass2", 2, "z", 98304, 2.8, 0.25),
    ("pass3", 2, "z", 98304, 2.8, 0.25),
    ("gelu", 2, "z", 98304, 2.8, 0.5),
    ("hand1", 2, "z", 98304, 2.8, 0.0),
    ("hand2", 2, "z", 98304, 2.8, 0.0),
    ("hand3", 2, "z", 49152, 2.8, 0.0),
    ("down", 3, "y", 98304, 2.7, 0.9),
    ("finish", 4, "x", 49152, 2.7, 0.4),
)
RATE = 50000.0
LOADED = {"project": 24.0, "up": 42.0, "down": 62.0}


def issue_order():
    chains = [[("spread", 7, "z", 393216, 4.3, 0.0, 0)] + [st + (0,) for st in CHAIN]]
    chains += [[st + (s,) for st in CHAIN] for s in range(1, S)]
    for g, members in enumerate(GROUPS):
        chains.append([("ctx%d" % t, 2, "z", 49152 * len(members) * (0.5 if t == 3 else 1), 2.8, 0.0, g) for t in range(4)])
    waits = {s: S + g for g, members in enumerate(GROUPS) for s in members}
    place, ready = [0] * len(chains), [16.0] * len(chains)
    for s in range(1, S):
        ready[s] = float("inf")
    free, now, order = {"z": 0.0, "y": 0.0, "x": 0.0}, 0.0, []
    while any(p < len(ch) for p, ch in zip(place, chains)):
        live = [i for i in range(len(chains)) if place[i] < len(chains[i])]
        due_at = {i: max(ready[i], LOADED.get(chains[i][place[i]][0], 0.0)) for i in live}
        first = min(due_at.values())
        i = min(i for i in live if due_at[i] <= max(now, first))
        name, copies, link, size, latency, work, index = chains[i][place[i]]
        now = max(now, due_at[i]) + work + 0.08 * copies
        free[link] = max(free[link], now) + size / RATE
        ready[i] = free[link] + latency
        place[i] += 1
        order.append((name, index))
        if i >= S and place[i] == len(chains[i]):
            for s, chain in waits.items():
                if chain == i:
                    ready[s] = ready[i]
    return order, max(ready[:S])


def kernel(ctx, res, wp, pb, ng, ns, wu, ub, wd, db, out,
           ctx_all, wproj, wup, wdown, resb, vin0, vin1, vin2, vin3, uin, vec, uvec, att, rs, mixed, st, nrm, prep, zr, hid,
           outp, os, obuf, ssem, rsem, wssem, wrsem, csem, gsem, lsem):
    r, q = lax.axis_index("row"), lax.axis_index("col")
    z, c = r // 2, r % 2
    x, y = q // 4, q % 4
    sib = (z * 2 + 1 - c, q)

    def zi(d):
        return (z + d + NZ) % NZ

    def yi(d):
        return (y + d) % NY

    def zp(d):
        return (zi(d) * 2 + c, q)

    def xp(d):
        return (r, ((x + d) % NX) * 4 + y)

    def yp(d):
        return (r, x * 4 + yi(d))

    def rows(start, size):
        return pl.ds(pl.multiple_of(start, 16), size)

    def lanes(start, size):
        return pl.ds(pl.multiple_of(start, 128), size)

    def local(src, dst, sem):
        copy = pltpu.make_async_copy(src, dst, sem)
        copy.start()
        return copy

    sends = []

    def remote(src, dst, send, recv, device):
        copy = pltpu.make_async_remote_copy(
            src_ref=src, dst_ref=dst, send_sem=send, recv_sem=recv, device_id=device, device_id_type=MESH
        )
        copy.start()
        sends.append((None, copy))
        return copy

    def give(src, dst, send, recv, to_core, to_x):
        here = (to_core == c) & (to_x == x)
        copy = pltpu.make_async_remote_copy(
            src_ref=src, dst_ref=dst, send_sem=send, recv_sem=recv, device_id=(z * 2 + to_core, to_x * 4 + y),
            device_id_type=MESH,
        )

        @pl.when(here)
        def _():
            pltpu.make_async_copy(src, dst, recv).start()

        @pl.when(jnp.logical_not(here))
        def _():
            copy.start()

        sends.append((here, copy))

    def clear(keep):
        while len(sends) > keep:
            here, copy = sends.pop(0)
            if here is None:
                copy.wait_send()
            else:
                pl.when(jnp.logical_not(here))(copy.wait_send)

    def landed(ref, sem):
        pltpu.make_async_copy(ref, ref, sem).wait()

    vin = (vin0, vin1, vin2, vin3)
    half = lanes(c * F, F)
    places = {
        "proj": lambda at, core: wproj.at[rows(at * F, F), lanes(core * F, F)],
        "up": lambda at, core: wup.at[rows(core * F, F), lanes(at * 2 * F, 2 * F)],
        "down": lambda at, core: wdown.at[rows(at * 2 * F, 2 * F), lanes(core * F, F)],
    }
    blocks = {"proj": wp, "up": wu, "down": wd}
    vector_in = [local(v, vin[i], lsem.at[i]) for i, v in enumerate((pb, ng, ns, db))] + [local(ub, uin, lsem.at[4])]
    own = {name: local(blocks[name], places[name](x, c), lsem.at[5 + i]) for i, name in enumerate(blocks)}

    barrier = pltpu.get_barrier_semaphore()
    partners = [sib] + [zp(d) for d in range(1, NZ)] + [yp(d) for d in range(1, NY)]
    partners += [p for d in range(1, NX) for p in (xp(d), (sib[0], xp(d)[1]))]
    for p in partners:
        pl.semaphore_signal(barrier, inc=1, device_id=p, device_id_type=MESH)
    pl.semaphore_wait(barrier, len(partners))

    ctx_side = (c + z // 2) % 2
    for g, (low, size) in enumerate(((0, T), (T, H - T))):
        for i in range(2):
            for core in range(2):
                give(ctx.at[rows(128 * core + 64 * i + low, size)], ctx_all.at[z, low:low + size, lanes(x * F, F)],
                     gsem.at[g * 4 + i * 2 + core], csem.at[g], core, 2 * ctx_side + i)
    gathers = {}

    def swap(name, i, src, dst):
        return remote(src, dst, wssem.at[i], wrsem.at[i], sib)

    def gather(name, i):
        mine = places[name](x, c)
        gathers[name] = (
            [remote(blocks[name], mine, wssem.at[8 * i + d], wrsem.at[8 * i + d], xp(d)) for d in (1, 3)],
            [swap(name, 8 * i, blocks[name], mine)],
            [],
            8 * i,
        )

    gather("proj", 0)
    side = (x + y) % 2
    for i in range(2):
        for core in range(2):
            give(res.at[rows(128 * core + 64 * i, H)], resb.at[c, x // 2], gsem.at[8 + i * 2 + core], csem.at[2], core, 2 * side + i)
    for copy in vector_in:
        copy.wait()
    for i in range(4):
        vec[c, i:i + 1, :] = vin[i][...].reshape(1, F).astype(jnp.float32)
    uvec[x, 0:1, :] = uin[...].reshape(1, 2 * F).astype(jnp.float32)
    vec_swap = [swap("vec", 24, vec.at[c], vec.at[c])]
    uvec_gather = [remote(uvec.at[x], uvec.at[x], wssem.at[24 + d], wrsem.at[24 + d], xp(d)) for d in (1, 3, 2)]

    def pass_on(name):
        near, far, relays, i = gathers[name]
        if not relays:
            for copy in near:
                copy.wait_recv()
            for j, (d, to) in enumerate(((-1, 1), (1, 3))):
                place = places[name]((x + d + NX) % NX, c)
                n = place.shape[0] // 2
                piece = place.at[j * n:(j + 1) * n]
                relays.append(remote(piece, piece, wssem.at[i + 4 + j], wrsem.at[i + 4 + j], xp(to)))
            for j, d in enumerate((-1, 1)):
                place = places[name]((x + d + NX) % NX, c)
                far.append(swap(name, i + (2, 6)[j], place, place))

    def pass_far(name):
        near, far, relays, i = gathers[name]
        if len(far) == 3:
            for copy in relays:
                copy.wait_recv()
            place = places[name]((x + 2) % NX, c)
            far.append(swap(name, i + 7, place, place))

    def ready(name):
        if name in gathers:
            pass_on(name)
            pass_far(name)
            own[name].wait()
            for copy in gathers.pop(name)[1]:
                copy.wait_recv()

    flights, slots = {}, {}

    def send(name, s, moves):
        copies = []
        for src, dst, device in moves:
            i = slots[s] = slots.get(s, -1) + 1
            copies.append(remote(src, dst, ssem.at[s, i], rsem.at[s, i], device))
        flights[name, s] = copies

    def arrive(name, s):
        for copy in flights.pop((name, s), ()):
            copy.wait_recv()

    def part(s):
        return slice(s * T, (s + 1) * T)

    def low(at):
        return 2 * ((x // 2 + at) % 2) + at // 2

    def spread(s):
        landed(ctx_all.at[z, 0:T], csem.at[0])
        piece = ctx_all.at[z, part(0), :]
        send("spread", 0, [(piece, piece, zp(d)) for d in (4, 3, 5, 2, 6, 1, 7)])

    def ring(t):
        def step(g):
            members = GROUPS[g]
            span = slice(members[0] * T, (members[-1] + 1) * T)
            if t == 0:
                if g == 0:
                    landed(ctx_all.at[z, T:H], csem.at[1])
            else:
                arrive("ctx%d" % (t - 1), S + g)
            cols = (slice(0, K // 2), slice(K // 2, K)) if t == 3 else (slice(0, K), slice(0, K))
            up_piece, down_piece = ctx_all.at[zi(-t), span, cols[0]], ctx_all.at[zi(t), span, cols[1]]
            send("ctx%d" % t, S + g, [(up_piece, up_piece, zp(1)), (down_piece, down_piece, zp(-1))])
        return step

    def scatter(name, s, product, piece, landing):
        k = part(s)
        piece[:, :, k, :] = product.astype(jnp.bfloat16).reshape(2, 4, T, 2 * F)
        send(name, s, [(piece.at[:, low(yi(d)), k, :], landing.at[d - 1, :, k, :], yp(d)) for d in (1, 3, 2)])

    def scattered(name, s, piece, landing):
        arrive(name, s)
        k = part(s)
        total = piece[:, low(y), k, :].astype(jnp.float32)
        for d in range(3):
            total = total + landing[d, :, k, :].astype(jnp.float32)
        return total.reshape(2 * T, 2 * F)

    def project(s):
        if s == 0:
            pass_on("proj")
            gather("up", 1)
            arrive("spread", 0)
        else:
            arrive("ctx3", S + [s in members for members in GROUPS].index(True))
        ready("proj")
        product = jnp.dot(ctx_all[:, part(s), :].reshape(NZ * T, K), wproj[...], preferred_element_type=jnp.float32)
        scatter("project", s, product, att, rs)

    def mix(s):
        total = scattered("project", s, att, rs)
        k = part(s)
        if s == 0:
            landed(resb, csem.at[2])
            vec_swap[0].wait_recv()
        row_sum, row_square = jnp.zeros((2 * T, 128), jnp.float32), jnp.zeros((2 * T, 128), jnp.float32)
        for h in range(2):
            value = resb[h, :, k, :].reshape(2 * T, F).astype(jnp.float32) + total[:, h * F:(h + 1) * F] + vec[h, 0:1, :]
            mixed[h, s] = value
            for i in range(0, F, 128):
                row_sum = row_sum + value[:, i:i + 128]
                row_square = row_square + value[:, i:i + 128] * value[:, i:i + 128]
        pad = jnp.zeros((64 - 2 * T, 128), jnp.float32)
        by_lane = jnp.concatenate([row_sum, pad, row_square, pad], axis=0).T
        st[s, z] = jnp.sum(by_lane, axis=0, keepdims=True)
        send("mix", s, [(st.at[s, z], st.at[s, z], zp(d)) for d in (4, 3, 5, 2, 6, 1, 7)])

    def norm(s):
        arrive("mix", s)
        k = part(s)
        total = jnp.broadcast_to(jnp.sum(st[s], axis=0), (128, 128)).T
        mean = total[0:2 * T, 0:1] / D
        var = total[64:64 + 2 * T, 0:1] / D - mean * mean
        scale = lax.rsqrt(var + 1e-05)
        for h in range(2):
            normed = (mixed[h, s] - mean) * scale * vec[h, 1:2, :] + vec[h, 2:3, :]
            nrm[:, low(y), k, h * F:(h + 1) * F] = normed.astype(jnp.bfloat16).reshape(2, T, F)
        piece = nrm.at[:, low(y), k, :]
        send("norm", s, [(piece, piece, yp(d)) for d in (1, 3, 2)])
        if s == 0:
            pass_on("up")
            gather("down", 2)

    def up(s):
        arrive("norm", s)
        ready("up")
        k = part(s)
        product = jnp.dot(nrm[:, :, k, :].reshape(NZ * T, 2 * F), wup[...], preferred_element_type=jnp.float32)
        prep[:, k, :] = product.astype(jnp.bfloat16).reshape(NZ, T, U)
        send("up", s, [
            (prep.at[zi(4), k, 0:U // 2], zr.at[0, 0, k, 0:U // 2], zp(1)),
            (prep.at[zi(4), k, U // 2:U], zr.at[1, 0, k, U // 2:U], zp(-1)),
        ])

    def passing(t):
        def step(s):
            arrive("up" if t == 1 else "pass%d" % (t - 1), s)
            k, moves = part(s), []
            for way, sign in ((0, 1), (1, -1)):
                at = zi(sign * (4 - t))
                cols = slice(0, U) if t > 1 else slice(way * (U // 2), (way + 1) * (U // 2))
                prep[at, k, cols] = (
                    prep[at, k, cols].astype(jnp.float32) + zr[way, t - 1, k, cols].astype(jnp.float32)
                ).astype(jnp.bfloat16)
                moves.append((prep.at[at, k, :], zr.at[way, t, k, :], zp(sign)))
            send("pass%d" % t, s, moves)
        return step

    def gelu(s):
        arrive("pass3", s)
        if s == 0:
            for copy in uvec_gather:
                copy.wait_recv()
        k = part(s)
        for i in range(NX):
            cols = slice(i * 2 * F, (i + 1) * 2 * F)
            total = prep[z, k, cols].astype(jnp.float32) + zr[0, 3, k, cols].astype(jnp.float32)
            total = total + zr[1, 3, k, cols].astype(jnp.float32) + uvec[i, 0:1, :]
            hid[z, k, cols] = jax.nn.gelu(total, approximate=True).astype(jnp.bfloat16)
        piece = hid.at[z, k, :]
        send("gelu", s, [(piece, piece, zp(1)), (piece, piece, zp(-1))])

    def handing(t):
        def step(s):
            arrive("gelu" if t == 1 else "hand%d" % (t - 1), s)
            cols = (slice(0, U // 2), slice(U // 2, U)) if t == 3 else (slice(0, U), slice(0, U))
            up_piece, down_piece = hid.at[zi(-t), part(s), cols[0]], hid.at[zi(t), part(s), cols[1]]
            send("hand%d" % t, s, [(up_piece, up_piece, zp(1)), (down_piece, down_piece, zp(-1))])
            if t == 1 and s == 0:
                pass_on("down")
        return step

    def down(s):
        arrive("hand3", s)
        ready("down")
        product = jnp.dot(hid[:, part(s), :].reshape(NZ * T, U), wdown[...], preferred_element_type=jnp.float32)
        scatter("down", s, product, outp, os)

    def finish(s):
        total = scattered("down", s, outp, os)
        for h in range(2):
            value = mixed[h, s] + total[:, h * F:(h + 1) * F] + vec[h, 3:4, :]
            obuf[h, s] = value.astype(jnp.bfloat16)
        for h in range(2):
            for k in range(2):
                give(obuf.at[h, s, k * T:(k + 1) * T], out.at[rows(128 * c + 64 * (x % 2) + s * T, T)],
                     gsem.at[12 + s * 4 + h * 2 + k], csem.at[3], h, (x // 2 + y) % 2 + 2 * k)

    stages = dict(spread=spread, project=project, mix=mix, norm=norm, up=up, gelu=gelu, down=down, finish=finish)
    for t in range(1, 4):
        stages["pass%d" % t], stages["hand%d" % t] = passing(t), handing(t)
    for t in range(4):
        stages["ctx%d" % t] = ring(t)
    for name, index in issue_order()[0]:
        stages[name](index)
        clear(40)
    clear(0)
    landed(out, csem.at[3])


def layer(context, residual_in, proj_weight, proj_bias, norm_gain, norm_shift, up_weight, up_bias, down_weight, down_bias):
    bf16, f32 = jnp.bfloat16, jnp.float32
    hbm = pl.BlockSpec(memory_space=pl.ANY)
    dma = pltpu.SemaphoreType.DMA
    return pl.pallas_call(
        kernel,
        out_shape=jax.ShapeDtypeStruct((256, F), bf16),
        in_specs=[hbm] * 10,
        out_specs=hbm,
        scratch_shapes=[
            pltpu.VMEM((NZ, H, K), bf16),
            pltpu.VMEM((K, 2 * F), bf16),
            pltpu.VMEM((2 * F, U), bf16),
            pltpu.VMEM((U, 2 * F), bf16),
            pltpu.VMEM((2, 2, H, F), bf16),
            *[pltpu.VMEM((F,), bf16)] * 4,
            pltpu.VMEM((2 * F,), bf16),
            pltpu.VMEM((2, 8, F), f32),
            pltpu.VMEM((NX, 8, 2 * F), f32),
            pltpu.VMEM((2, 4, H, 2 * F), bf16),
            pltpu.VMEM((3, 2, H, 2 * F), bf16),
            pltpu.VMEM((2, S, 2 * T, F), f32),
            pltpu.VMEM((S, NZ, 1, 128), f32),
            pltpu.VMEM((2, 4, H, 2 * F), bf16),
            pltpu.VMEM((NZ, H, U), bf16),
            pltpu.VMEM((2, 4, H, U), bf16),
            pltpu.VMEM((NZ, H, U), bf16),
            pltpu.VMEM((2, 4, H, 2 * F), bf16),
            pltpu.VMEM((3, 2, H, 2 * F), bf16),
            pltpu.VMEM((2, S, 2 * T, F), bf16),
            dma((S + len(GROUPS), 44)),
            dma((S + len(GROUPS), 44)),
            dma((28,)),
            dma((28,)),
            dma((4,)),
            dma((12 + 4 * S,)),
            dma((8,)),
        ],
        compiler_params=pltpu.CompilerParams(
            collective_id=0, has_side_effects=True, vmem_limit_bytes=56 * 2**20
        ),
        name="layer",
    )(context, residual_in, proj_weight, proj_bias, norm_gain, norm_shift, up_weight, up_bias, down_weight, down_bias)


def solution(mesh):
    return jax.shard_map(
        layer,
        mesh=mesh,
        in_specs=(
            P("row", "col"),
            P("col", "row"),
            P("col", "row"),
            P("row"),
            P("row"),
            P("row"),
            P("row", "col"),
            P("col"),
            P("col", "row"),
            P("row"),
        ),
        out_specs=P("col", "row"),
        check_vma=False,
    )
```

```python
import jax
import jax.numpy as jnp
from jax import lax
from jax.experimental import pallas as pl
from jax.experimental.pallas import tpu as pltpu
from jax.sharding import PartitionSpec as P

D = 6144
F = 384
K = 4 * F
U = 8 * F
H = 64
S = 4
T = H // S
GROUPS = ((1,), (2, 3))
NZ, NX, NY = 8, 4, 4
MESH = pl.DeviceIdType.MESH

PARTS = (((0, 3 * U // 4), (3 * U // 4, U)),) + (((0, U),),) * (S - 1)
RATE = 50000.0
Z_STEPS = ("up", "pass1", "pass2", "pass3", "gelu", "hand1", "hand2", "hand3")
Z_WORK = dict(up=0.9, pass1=0.25, pass2=0.25, pass3=0.25, gelu=0.5)


def issue_order():
    nodes = {
        ("relay_proj", 0, 0): ((), 16.5, 0.0, 4, "x", 0, 0.0),
        ("share_proj", 0, 0): ((("relay_proj", 0, 0),), 20.0, 0.0, 2, "x", 0, 0.0),
        ("relay_up", 0, 0): ((("share_proj", 0, 0),), 32.0, 0.0, 4, "x", 0, 0.0),
        ("share_up", 0, 0): ((("relay_up", 0, 0),), 39.0, 0.0, 2, "x", 0, 0.0),
        ("relay_down", 0, 0): ((("share_up", 0, 0),), 52.0, 0.0, 4, "x", 0, 0.0),
        ("share_down", 0, 0): ((("relay_down", 0, 0),), 62.0, 0.0, 2, "x", 0, 0.0),
        ("spread", 0, 0): ((), 14.0, 0.0, 7, "z", 393216, 4.3),
    }
    arrived = {0: ("spread", 0, 0)}
    for s in range(S):
        if s > 0:
            g = [s in members for members in GROUPS].index(True)
            arrived[s] = ("ctx3", g, 0)
        nodes["project", s, 0] = ((arrived[s],), 25.0, 0.6, 3, "y", 98304, 2.7)
        nodes["mix", s, 0] = ((("project", s, 0),), 0.0, 0.6, 7, "z", 0, 4.3)
        nodes["norm", s, 0] = ((("mix", s, 0),), 0.0, 0.5, 3, "y", 98304, 2.7)
        for u, (first_unit, last_unit) in enumerate(PARTS[s]):
            share = (last_unit - first_unit) / U
            before = ("norm", s, 0)
            for name in Z_STEPS:
                size = 98304 * share * (0.5 if name in ("up", "hand3") else 1)
                nodes[name, s, u] = ((before,), 46.0 if (name, u) == ("up", 1) else 0.0, Z_WORK.get(name, 0.0) * share, 2, "z", size, 2.8)
                before = (name, s, u)
        nodes["down", s, 0] = (tuple(("hand3", s, u) for u in range(len(PARTS[s]))), 0.0, 0.9, 3, "y", 98304, 2.7)
        nodes["finish", s, 0] = ((("down", s, 0),), 0.0, 0.4, 4, "x", 49152, 2.7)
    for g, members in enumerate(GROUPS):
        for t in range(4):
            size = 49152 * len(members) * (0.5 if t == 3 else 1)
            nodes["ctx%d" % t, g, 0] = (((("ctx%d" % (t - 1), g, 0),) if t else ()), 20.5 if t == 0 else 0.0, 0.0, 2, "z", size, 2.8)
    urgency = {node: (node[0].startswith("ctx"), node[1], node[2]) for node in nodes}
    free, now, order, done = {"z": 0.0, "y": 0.0, "x": 0.0}, 0.0, [], {}
    while len(order) < len(nodes):
        due = {
            node: max([start] + [done[n] for n in after])
            for node, (after, start, *_) in nodes.items()
            if node not in done and all(n in done for n in after)
        }
        first = min(due.values())
        node = min((n for n in due if due[n] <= max(now, first)), key=lambda n: (urgency[n], n))
        _, _, work, copies, link, size, latency = nodes[node]
        now = max(now, due[node]) + work + 0.06 * copies
        free[link] = max(free[link], now) + size / RATE
        done[node] = free[link] + latency
        order.append(node)
    return order, max(done.values())


def kernel(ctx, res, wp, pb, ng, ns, wu, ub, wd, db, out,
           ctx_all, wproj, wup, wdown, resb, vin0, vin1, vin2, vin3, uin, vec, uvec, att, rs, mixed, st, nrm, prep, zr, hid,
           outp, os, obuf, ssem, rsem, wssem, wrsem, csem, gsem, lsem):
    r, q = lax.axis_index("row"), lax.axis_index("col")
    z, c = r // 2, r % 2
    x, y = q // 4, q % 4
    sib = (z * 2 + 1 - c, q)

    def zi(d):
        return (z + d + NZ) % NZ

    def yi(d):
        return (y + d) % NY

    def zp(d):
        return (zi(d) * 2 + c, q)

    def xp(d):
        return (r, ((x + d) % NX) * 4 + y)

    def yp(d):
        return (r, x * 4 + yi(d))

    def rows(start, size):
        return pl.ds(pl.multiple_of(start, 16), size)

    def lanes(start, size):
        return pl.ds(pl.multiple_of(start, 128), size)

    def local(src, dst, sem):
        copy = pltpu.make_async_copy(src, dst, sem)
        copy.start()
        return copy

    sends = []

    def remote(src, dst, send, recv, device):
        copy = pltpu.make_async_remote_copy(
            src_ref=src, dst_ref=dst, send_sem=send, recv_sem=recv, device_id=device, device_id_type=MESH
        )
        copy.start()
        sends.append((None, copy))
        return copy

    def give(src, dst, send, recv, to_core, to_x):
        here = (to_core == c) & (to_x == x)
        copy = pltpu.make_async_remote_copy(
            src_ref=src, dst_ref=dst, send_sem=send, recv_sem=recv, device_id=(z * 2 + to_core, to_x * 4 + y),
            device_id_type=MESH,
        )

        @pl.when(here)
        def _():
            pltpu.make_async_copy(src, dst, recv).start()

        @pl.when(jnp.logical_not(here))
        def _():
            copy.start()

        sends.append((here, copy))

    def clear(keep):
        while len(sends) > keep:
            here, copy = sends.pop(0)
            if here is None:
                copy.wait_send()
            else:
                pl.when(jnp.logical_not(here))(copy.wait_send)

    def landed(ref, sem):
        pltpu.make_async_copy(ref, ref, sem).wait()

    vin = (vin0, vin1, vin2, vin3)
    half = lanes(c * F, F)
    places = {
        "proj": lambda slot: wproj.at[slot * F:(slot + 1) * F, half],
        "up": lambda slot: wup.at[rows(c * F, F), slot * 2 * F:(slot + 1) * 2 * F],
        "down": lambda slot: wdown.at[slot * 2 * F:(slot + 1) * 2 * F, half],
    }
    blocks = {"proj": wp, "up": wu, "down": wd}
    vector_in = [local(v, vin[i], lsem.at[i]) for i, v in enumerate((pb, ng, ns, db))] + [local(ub, uin, lsem.at[4])]
    own = {name: local(blocks[name], places[name](0), lsem.at[5 + i]) for i, name in enumerate(blocks)}

    barrier = pltpu.get_barrier_semaphore()
    partners = [sib] + [zp(d) for d in range(1, NZ)] + [yp(d) for d in range(1, NY)]
    partners += [p for d in range(1, NX) for p in (xp(d), (sib[0], xp(d)[1]))]
    for p in partners:
        pl.semaphore_signal(barrier, inc=1, device_id=p, device_id_type=MESH)
    pl.semaphore_wait(barrier, len(partners))

    gathers = {}

    def swap(name, i, src, dst):
        return remote(src, dst, wssem.at[i], wrsem.at[i], sib)

    def halves(place):
        n = place.shape[0] // 2
        return place.at[0:n], place.at[n:2 * n]

    def gather(name, i):
        block, near = halves(blocks[name]), {}
        for first in (True, False):
            for j, d in ((0, 1), (1, 3)):
                k = j if first else 1 - j
                n = i + 2 * j + (0 if first else 1)
                near[j, first] = remote(block[k], halves(places[name](1 + j))[k], wssem.at[n], wrsem.at[n], xp(d))
        gathers[name] = (near, [swap(name, i + 4, blocks[name], places[name](0))], [], i)

    ctx_side = (c + z // 2) % 2

    def slot_at(at):
        d = (x - at + NX) % NX
        return jnp.where(d == 3, 1, jnp.where(d == 0, 0, d + 1))

    def give_context(g, low, size):
        for i in range(2):
            for core in range(2):
                give(ctx.at[rows(128 * core + 64 * i + low, size)], ctx_all.at[z, low:low + size, lanes(slot_at(2 * ctx_side + i) * F, F)],
                     gsem.at[g * 4 + i * 2 + core], csem.at[g], core, 2 * ctx_side + i)

    def give_residual():
        side = (x + y) % 2
        for i in range(2):
            for core in range(2):
                give(res.at[rows(128 * core + 64 * i, H)], resb.at[c, x // 2], gsem.at[8 + i * 2 + core], csem.at[2],
                     core, 2 * side + i)

    give_context(0, 0, T)
    gather("proj", 0)
    give_context(1, T, H - T)
    for copy in vector_in:
        copy.wait()
    for i in range(4):
        vec[c, i:i + 1, :] = vin[i][...].reshape(1, F).astype(jnp.float32)
    uvec[0, 0:1, :] = uin[...].reshape(1, 2 * F).astype(jnp.float32)
    vec_swap = [swap("vec", 30, vec.at[c], vec.at[c])]
    uvec_gather = [remote(uvec.at[0], uvec.at[{1: 1, 3: 2, 2: 3}[d]], wssem.at[30 + d], wrsem.at[30 + d], xp(d)) for d in (1, 3, 2)]

    def relay(name):
        near, far, relays, i = gathers[name]
        for j, to in ((0, 1), (1, 3)):
            near[j, True].wait_recv()
            piece, goal = halves(places[name](1 + j))[j], halves(places[name](3))[j]
            relays.append(remote(piece, goal, wssem.at[i + 5 + j], wrsem.at[i + 5 + j], xp(to)))

    def share(name):
        near, far, relays, i = gathers[name]
        for j in range(2):
            near[j, False].wait_recv()
            far.append(swap(name, i + 7 + j, places[name](1 + j), places[name](1 + j)))

    def ready(name, near_only=False):
        if name in own:
            own.pop(name).wait()
            for copy in gathers[name][1]:
                copy.wait_recv()
        if name in gathers and not near_only:
            near, far, relays, i = gathers.pop(name)
            for copy in relays:
                copy.wait_recv()
            swap(name, i + 9, places[name](3), places[name](3)).wait_recv()

    flights, slots = {}, {}

    def send(name, s, moves):
        copies = []
        for src, dst, device in moves:
            i = slots[s] = slots.get(s, -1) + 1
            copies.append(remote(src, dst, ssem.at[s, i], rsem.at[s, i], device))
        flights[name, s] = copies

    def arrive(name, s):
        for copy in flights.pop((name, s), ()):
            copy.wait_recv()

    def part(s):
        return slice(s * T, (s + 1) * T)

    def low(at):
        return 2 * ((x // 2 + at) % 2) + at // 2

    def spread(s):
        landed(ctx_all.at[z, 0:T], csem.at[0])
        piece = ctx_all.at[z, part(0), :]
        send("spread", 0, [(piece, piece, zp(d)) for d in (4, 3, 5, 2, 6, 1, 7)])

    def ring(t):
        def step(g):
            members = GROUPS[g]
            span = slice(members[0] * T, (members[-1] + 1) * T)
            if t == 0:
                if g == 0:
                    landed(ctx_all.at[z, T:H], csem.at[1])
            else:
                arrive("ctx%d" % (t - 1), S + g)
            cols = (slice(0, K // 2), slice(K // 2, K)) if t == 3 else (slice(0, K), slice(0, K))
            up_piece, down_piece = ctx_all.at[zi(-t), span, cols[0]], ctx_all.at[zi(t), span, cols[1]]
            send("ctx%d" % t, S + g, [(up_piece, up_piece, zp(1)), (down_piece, down_piece, zp(-1))])
        return step

    def scatter(name, s, product, piece, landing):
        k = part(s)
        piece[:, :, k, :] = product.astype(jnp.bfloat16).reshape(2, 4, T, 2 * F)
        send(name, s, [(piece.at[:, low(yi(d)), k, :], landing.at[d - 1, :, k, :], yp(d)) for d in (1, 3, 2)])

    def scattered(name, s, piece, landing):
        arrive(name, s)
        k = part(s)
        total = piece[:, low(y), k, :].astype(jnp.float32)
        for d in range(3):
            total = total + landing[d, :, k, :].astype(jnp.float32)
        return total.reshape(2 * T, 2 * F)

    def project(s):
        if s == 0:
            arrive("spread", 0)
        else:
            arrive("ctx3", S + [s in members for members in GROUPS].index(True))
        ready("proj")
        product = jnp.dot(ctx_all[:, part(s), :].reshape(NZ * T, K), wproj[...], preferred_element_type=jnp.float32)
        scatter("project", s, product, att, rs)

    def mix(s):
        total = scattered("project", s, att, rs)
        k = part(s)
        if s == 0:
            landed(resb, csem.at[2])
            vec_swap[0].wait_recv()
        row_sum, row_square = jnp.zeros((2 * T, 128), jnp.float32), jnp.zeros((2 * T, 128), jnp.float32)
        for h in range(2):
            value = resb[h, :, k, :].reshape(2 * T, F).astype(jnp.float32) + total[:, h * F:(h + 1) * F] + vec[h, 0:1, :]
            mixed[h, s] = value
            for i in range(0, F, 128):
                row_sum = row_sum + value[:, i:i + 128]
                row_square = row_square + value[:, i:i + 128] * value[:, i:i + 128]
        pad = jnp.zeros((64 - 2 * T, 128), jnp.float32)
        by_lane = jnp.concatenate([row_sum, pad, row_square, pad], axis=0).T
        st[s, z] = jnp.sum(by_lane, axis=0, keepdims=True)
        send("mix", s, [(st.at[s, z], st.at[s, z], zp(d)) for d in (4, 3, 5, 2, 6, 1, 7)])

    def norm(s):
        arrive("mix", s)
        k = part(s)
        total = jnp.broadcast_to(jnp.sum(st[s], axis=0), (128, 128)).T
        mean = total[0:2 * T, 0:1] / D
        var = total[64:64 + 2 * T, 0:1] / D - mean * mean
        scale = lax.rsqrt(var + 1e-05)
        for h in range(2):
            normed = (mixed[h, s] - mean) * scale * vec[h, 1:2, :] + vec[h, 2:3, :]
            nrm[:, low(y), k, h * F:(h + 1) * F] = normed.astype(jnp.bfloat16).reshape(2, T, F)
        piece = nrm.at[:, low(y), k, :]
        send("norm", s, [(piece, piece, yp(d)) for d in (1, 3, 2)])


    def columns(s, u):
        start, stop = PARTS[s][u]
        middle = (start + stop) // 2
        return slice(start, stop), (slice(start, middle), slice(middle, stop))

    def up(s, u):
        if u == 0:
            arrive("norm", s)
        ready("up", (s, u) == (0, 0))
        k, (cols, sides) = part(s), columns(s, u)
        product = jnp.dot(nrm[:, :, k, :].reshape(NZ * T, 2 * F), wup[:, cols], preferred_element_type=jnp.float32)
        prep[:, k, cols] = product.astype(jnp.bfloat16).reshape(NZ, T, cols.stop - cols.start)
        send(("up", u), s, [
            (prep.at[zi(4), k, sides[0]], zr.at[0, 0, k, sides[0]], zp(1)),
            (prep.at[zi(4), k, sides[1]], zr.at[1, 0, k, sides[1]], zp(-1)),
        ])

    def passing(t):
        def step(s, u):
            arrive(("up" if t == 1 else "pass%d" % (t - 1), u), s)
            k, (cols, sides), moves = part(s), columns(s, u), []
            for way, sign in ((0, 1), (1, -1)):
                at = zi(sign * (4 - t))
                came = cols if t > 1 else sides[way]
                prep[at, k, came] = (
                    prep[at, k, came].astype(jnp.float32) + zr[way, t - 1, k, came].astype(jnp.float32)
                ).astype(jnp.bfloat16)
                moves.append((prep.at[at, k, cols], zr.at[way, t, k, cols], zp(sign)))
            send(("pass%d" % t, u), s, moves)
        return step

    def gelu(s, u):
        arrive(("pass3", u), s)
        if (s, u) == (0, 0):
            for copy in uvec_gather:
                copy.wait_recv()
        k, (cols, _) = part(s), columns(s, u)
        for i in range(cols.start, cols.stop, F):
            at = slice(i, i + F)
            total = prep[z, k, at].astype(jnp.float32) + zr[0, 3, k, at].astype(jnp.float32)
            unit = i % (2 * F)
            total = total + zr[1, 3, k, at].astype(jnp.float32) + uvec[i // (2 * F), 0:1, unit:unit + F]
            hid[z, k, at] = jax.nn.gelu(total, approximate=True).astype(jnp.bfloat16)
        piece = hid.at[z, k, cols]
        send(("gelu", u), s, [(piece, piece, zp(1)), (piece, piece, zp(-1))])

    def handing(t):
        def step(s, u):
            arrive(("gelu" if t == 1 else "hand%d" % (t - 1), u), s)
            cols, sides = columns(s, u)
            ways = sides if t == 3 else (cols, cols)
            up_piece, down_piece = hid.at[zi(-t), part(s), ways[0]], hid.at[zi(t), part(s), ways[1]]
            send(("hand%d" % t, u), s, [(up_piece, up_piece, zp(1)), (down_piece, down_piece, zp(-1))])
        return step

    def down(s):
        for u in range(len(PARTS[s])):
            arrive(("hand3", u), s)
        ready("down")
        product = jnp.dot(hid[:, part(s), :].reshape(NZ * T, U), wdown[...], preferred_element_type=jnp.float32)
        scatter("down", s, product, outp, os)

    def finish(s):
        total = scattered("down", s, outp, os)
        for h in range(2):
            value = mixed[h, s] + total[:, h * F:(h + 1) * F] + vec[h, 3:4, :]
            obuf[h, s] = value.astype(jnp.bfloat16)
        for h in range(2):
            for k in range(2):
                give(obuf.at[h, s, k * T:(k + 1) * T], out.at[rows(128 * c + 64 * (x % 2) + s * T, T)],
                     gsem.at[12 + s * 4 + h * 2 + k], csem.at[3], h, (x // 2 + y) % 2 + 2 * k)

    stages = {("spread", "project", "mix", "norm", "down", "finish")[i]: f
              for i, f in enumerate((spread, project, mix, norm, down, finish))}
    for t in range(4):
        stages["ctx%d" % t] = ring(t)
    by_part = dict(up=up, gelu=gelu)
    for t in range(1, 4):
        by_part["pass%d" % t], by_part["hand%d" % t] = passing(t), handing(t)
    for name, s, u in issue_order()[0]:
        if name in by_part:
            by_part[name](s, u)
        elif name == "relay_proj":
            relay("proj")
            give_residual()
            gather("up", 10)
        elif name == "relay_up":
            relay("up")
            gather("down", 20)
        elif name == "relay_down":
            relay("down")
        elif name.startswith("share_"):
            share(name[6:])
        else:
            stages[name](s)
        clear(60)
    clear(0)
    landed(out, csem.at[3])


def layer(context, residual_in, proj_weight, proj_bias, norm_gain, norm_shift, up_weight, up_bias, down_weight, down_bias):
    bf16, f32 = jnp.bfloat16, jnp.float32
    hbm = pl.BlockSpec(memory_space=pl.ANY)
    dma = pltpu.SemaphoreType.DMA
    return pl.pallas_call(
        kernel,
        out_shape=jax.ShapeDtypeStruct((256, F), bf16),
        in_specs=[hbm] * 10,
        out_specs=hbm,
        scratch_shapes=[
            pltpu.VMEM((NZ, H, K), bf16),
            pltpu.VMEM((K, 2 * F), bf16),
            pltpu.VMEM((2 * F, U), bf16),
            pltpu.VMEM((U, 2 * F), bf16),
            pltpu.VMEM((2, 2, H, F), bf16),
            *[pltpu.VMEM((F,), bf16)] * 4,
            pltpu.VMEM((2 * F,), bf16),
            pltpu.VMEM((2, 8, F), f32),
            pltpu.VMEM((NX, 8, 2 * F), f32),
            pltpu.VMEM((2, 4, H, 2 * F), bf16),
            pltpu.VMEM((3, 2, H, 2 * F), bf16),
            pltpu.VMEM((2, S, 2 * T, F), f32),
            pltpu.VMEM((S, NZ, 1, 128), f32),
            pltpu.VMEM((2, 4, H, 2 * F), bf16),
            pltpu.VMEM((NZ, H, U), bf16),
            pltpu.VMEM((2, 4, H, U), bf16),
            pltpu.VMEM((NZ, H, U), bf16),
            pltpu.VMEM((2, 4, H, 2 * F), bf16),
            pltpu.VMEM((3, 2, H, 2 * F), bf16),
            pltpu.VMEM((2, S, 2 * T, F), bf16),
            dma((S + len(GROUPS), 56)),
            dma((S + len(GROUPS), 56)),
            dma((34,)),
            dma((34,)),
            dma((4,)),
            dma((12 + 4 * S,)),
            dma((8,)),
        ],
        compiler_params=pltpu.CompilerParams(
            collective_id=0, has_side_effects=True, vmem_limit_bytes=56 * 2**20
        ),
        name="layer",
    )(context, residual_in, proj_weight, proj_bias, norm_gain, norm_shift, up_weight, up_bias, down_weight, down_bias)


def solution(mesh):
    return jax.shard_map(
        layer,
        mesh=mesh,
        in_specs=(
            P("row", "col"),
            P("col", "row"),
            P("col", "row"),
            P("row"),
            P("row"),
            P("row"),
            P("row", "col"),
            P("col"),
            P("col", "row"),
            P("row"),
        ),
        out_specs=P("col", "row"),
        check_vma=False,
    )
```

```python
import jax
import jax.numpy as jnp
from jax import lax
from jax.experimental import pallas as pl
from jax.experimental.pallas import tpu as pltpu
from jax.sharding import PartitionSpec as P

D = 6144
F = 384
K = 4 * F
U = 8 * F
H = 64
S = 4
T = H // S
GROUPS = ((1,), (2, 3))
NZ, NX, NY = 8, 4, 4
MESH = pl.DeviceIdType.MESH

PARTS = (((0, 3 * U // 4), (3 * U // 4, U)),) + (((0, U),),) * (S - 1)
RATE = 50000.0
Z_STEPS = ("up", "pass1", "pass2", "pass3", "gelu", "hand1", "hand2", "hand3")
Z_WORK = dict(up=0.9, pass1=0.25, pass2=0.25, pass3=0.25, gelu=0.5)


def issue_order():
    nodes = {
        ("relay_proj", 0, 0): ((), 16.5, 0.0, 4, "x", 0, 0.0),
        ("share_proj", 0, 0): ((("relay_proj", 0, 0),), 20.0, 0.0, 2, "x", 0, 0.0),
        ("relay_up", 0, 0): ((("share_proj", 0, 0),), 34.5, 0.0, 4, "x", 0, 0.0),
        ("share_up", 0, 0): ((("relay_up", 0, 0),), 41.0, 0.0, 2, "x", 0, 0.0),
        ("relay_down", 0, 0): ((("share_up", 0, 0),), 62.0, 0.0, 4, "x", 0, 0.0),
        ("share_down", 0, 0): ((("relay_down", 0, 0),), 75.0, 0.0, 2, "x", 0, 0.0),
        ("spread", 0, 0): ((), 14.0, 0.0, 7, "z", 393216, 4.3),
    }
    arrived = {0: ("spread", 0, 0)}
    for s in range(S):
        if s > 0:
            g = [s in members for members in GROUPS].index(True)
            arrived[s] = ("ctx3", g, 0)
        nodes["project", s, 0] = ((arrived[s],), 25.0, 0.6, 3, "y", 98304, 2.7)
        nodes["mix", s, 0] = ((("project", s, 0),), 0.0, 0.6, 7, "z", 0, 4.3)
        nodes["norm", s, 0] = ((("mix", s, 0),), 0.0, 0.5, 3, "y", 98304, 2.7)
        for u, (first_unit, last_unit) in enumerate(PARTS[s]):
            share = (last_unit - first_unit) / U
            before = ("norm", s, 0)
            for name in Z_STEPS:
                size = 98304 * share * (0.5 if name in ("up", "hand3") else 1)
                nodes[name, s, u] = ((before,), 50.0 if (name, u) == ("up", 1) else 0.0, Z_WORK.get(name, 0.0) * share, 2, "z", size, 2.8)
                before = (name, s, u)
        nodes["down", s, 0] = (tuple(("hand3", s, u) for u in range(len(PARTS[s]))), 0.0, 0.9, 3, "y", 98304, 2.7)
        nodes["finish", s, 0] = ((("down", s, 0),), 0.0, 0.4, 4, "x", 49152, 2.7)
    for g, members in enumerate(GROUPS):
        for t in range(4):
            size = 49152 * len(members) * (0.5 if t == 3 else 1)
            nodes["ctx%d" % t, g, 0] = (((("ctx%d" % (t - 1), g, 0),) if t else ()), 20.5 if t == 0 else 0.0, 0.0, 2, "z", size, 2.8)
    urgency = {node: (node[0].startswith("ctx"), node[1], node[2]) for node in nodes}
    free, now, order, done = {"z": 0.0, "y": 0.0, "x": 0.0}, 0.0, [], {}
    while len(order) < len(nodes):
        due = {
            node: max([start] + [done[n] for n in after])
            for node, (after, start, *_) in nodes.items()
            if node not in done and all(n in done for n in after)
        }
        first = min(due.values())
        node = min((n for n in due if due[n] <= max(now, first)), key=lambda n: (urgency[n], n))
        _, _, work, copies, link, size, latency = nodes[node]
        now = max(now, due[node]) + work + 0.06 * copies
        free[link] = max(free[link], now) + size / RATE
        done[node] = free[link] + latency
        order.append(node)
    return order, max(done.values())


def kernel(ctx, res, wp, pb, ng, ns, wu, ub, wd, db, out,
           ctx_all, wproj, wup, wdown, resb, vin0, vin1, vin2, vin3, uin, vec, uvec, att, rs, mixed, st, nrm, prep, zr, hid,
           outp, os, obuf, ssem, rsem, wssem, wrsem, csem, gsem, lsem):
    r, q = lax.axis_index("row"), lax.axis_index("col")
    z, c = r // 2, r % 2
    x, y = q // 4, q % 4
    sib = (z * 2 + 1 - c, q)

    def zi(d):
        return (z + d + NZ) % NZ

    def yi(d):
        return (y + d) % NY

    def zp(d):
        return (zi(d) * 2 + c, q)

    def xp(d):
        return (r, ((x + d) % NX) * 4 + y)

    def yp(d):
        return (r, x * 4 + yi(d))

    def rows(start, size):
        return pl.ds(pl.multiple_of(start, 16), size)

    def lanes(start, size):
        return pl.ds(pl.multiple_of(start, 128), size)

    def local(src, dst, sem):
        copy = pltpu.make_async_copy(src, dst, sem)
        copy.start()
        return copy

    sends = []

    def remote(src, dst, send, recv, device):
        copy = pltpu.make_async_remote_copy(
            src_ref=src, dst_ref=dst, send_sem=send, recv_sem=recv, device_id=device, device_id_type=MESH
        )
        copy.start()
        sends.append((None, copy))
        return copy

    def give(src, dst, send, recv, to_core, to_x):
        here = (to_core == c) & (to_x == x)
        copy = pltpu.make_async_remote_copy(
            src_ref=src, dst_ref=dst, send_sem=send, recv_sem=recv, device_id=(z * 2 + to_core, to_x * 4 + y),
            device_id_type=MESH,
        )

        @pl.when(here)
        def _():
            pltpu.make_async_copy(src, dst, recv).start()

        @pl.when(jnp.logical_not(here))
        def _():
            copy.start()

        sends.append((here, copy))

    def clear(keep):
        while len(sends) > keep:
            here, copy = sends.pop(0)
            if here is None:
                copy.wait_send()
            else:
                pl.when(jnp.logical_not(here))(copy.wait_send)

    def landed(ref, sem):
        pltpu.make_async_copy(ref, ref, sem).wait()

    vin = (vin0, vin1, vin2, vin3)
    half = lanes(c * F, F)
    places = {
        "proj": lambda slot: wproj.at[slot * F:(slot + 1) * F, half],
        "up": lambda slot: wup.at[rows(c * F, F), slot * 2 * F:(slot + 1) * 2 * F],
        "down": lambda slot: wdown.at[slot * 2 * F:(slot + 1) * 2 * F, half],
    }
    blocks = {"proj": wp, "up": wu, "down": wd}
    vector_in = [local(v, vin[i], lsem.at[i]) for i, v in enumerate((pb, ng, ns, db))] + [local(ub, uin, lsem.at[4])]
    own = {name: local(blocks[name], places[name](0), lsem.at[5 + i]) for i, name in enumerate(blocks)}

    barrier = pltpu.get_barrier_semaphore()
    partners = [sib] + [zp(d) for d in range(1, NZ)] + [yp(d) for d in range(1, NY)]
    partners += [p for d in range(1, NX) for p in (xp(d), (sib[0], xp(d)[1]))]
    for p in partners:
        pl.semaphore_signal(barrier, inc=1, device_id=p, device_id_type=MESH)
    pl.semaphore_wait(barrier, len(partners))

    gathers = {}

    def swap(name, i, src, dst):
        return remote(src, dst, wssem.at[i], wrsem.at[i], sib)

    def halves(place):
        n = place.shape[0] // 2
        return place.at[0:n], place.at[n:2 * n]

    def gather(name, i):
        block, near = halves(blocks[name]), {}
        for first in (True, False):
            for j, d in ((0, 1), (1, 3)):
                k = j if first else 1 - j
                n = i + 2 * j + (0 if first else 1)
                near[j, first] = remote(block[k], halves(places[name](1 + j))[k], wssem.at[n], wrsem.at[n], xp(d))
        gathers[name] = (near, [swap(name, i + 4, blocks[name], places[name](0))], [], i)

    ctx_side = (c + z // 2) % 2

    def slot_at(at):
        d = (x - at + NX) % NX
        return jnp.where(d == 3, 1, jnp.where(d == 0, 0, d + 1))

    def give_context(g, low, size):
        for i in range(2):
            for core in range(2):
                give(ctx.at[rows(128 * core + 64 * i + low, size)], ctx_all.at[z, low:low + size, lanes(slot_at(2 * ctx_side + i) * F, F)],
                     gsem.at[g * 4 + i * 2 + core], csem.at[g], core, 2 * ctx_side + i)

    def give_residual():
        side = (x + y) % 2
        for i in range(2):
            for core in range(2):
                give(res.at[rows(128 * core + 64 * i, H)], resb.at[c, x // 2], gsem.at[8 + i * 2 + core], csem.at[2],
                     core, 2 * side + i)

    give_context(0, 0, T)
    gather("proj", 0)
    give_context(1, T, H - T)
    for copy in vector_in:
        copy.wait()
    for i in range(4):
        vec[c, i:i + 1, :] = vin[i][...].reshape(1, F).astype(jnp.float32)
    uvec[0, 0:1, :] = uin[...].reshape(1, 2 * F).astype(jnp.float32)
    vec_swap = [swap("vec", 30, vec.at[c], vec.at[c])]
    uvec_gather = [remote(uvec.at[0], uvec.at[{1: 1, 3: 2, 2: 3}[d]], wssem.at[30 + d], wrsem.at[30 + d], xp(d)) for d in (1, 3, 2)]

    def relay(name):
        near, far, relays, i = gathers[name]
        for j, to in ((0, 1), (1, 3)):
            near[j, True].wait_recv()
            piece, goal = halves(places[name](1 + j))[j], halves(places[name](3))[j]
            relays.append(remote(piece, goal, wssem.at[i + 5 + j], wrsem.at[i + 5 + j], xp(to)))

    def share(name):
        near, far, relays, i = gathers[name]
        for j in range(2):
            near[j, False].wait_recv()
            far.append(swap(name, i + 7 + j, places[name](1 + j), places[name](1 + j)))

    def ready(name, near_only=False):
        if name in own:
            own.pop(name).wait()
            for copy in gathers[name][1]:
                copy.wait_recv()
        if name in gathers and not near_only:
            near, far, relays, i = gathers.pop(name)
            for copy in relays:
                copy.wait_recv()
            swap(name, i + 9, places[name](3), places[name](3)).wait_recv()

    flights, slots = {}, {}

    def send(name, s, moves):
        copies = []
        for src, dst, device in moves:
            i = slots[s] = slots.get(s, -1) + 1
            copies.append(remote(src, dst, ssem.at[s, i], rsem.at[s, i], device))
        flights[name, s] = copies

    def arrive(name, s):
        for copy in flights.pop((name, s), ()):
            copy.wait_recv()

    def part(s):
        return slice(s * T, (s + 1) * T)

    def low(at):
        return 2 * ((x // 2 + at) % 2) + at // 2

    def spread(s):
        landed(ctx_all.at[z, 0:T], csem.at[0])
        piece = ctx_all.at[z, part(0), :]
        send("spread", 0, [(piece, piece, zp(d)) for d in (4, 3, 5, 2, 6, 1, 7)])

    def ring(t):
        def step(g):
            members = GROUPS[g]
            span = slice(members[0] * T, (members[-1] + 1) * T)
            if t == 0:
                if g == 0:
                    landed(ctx_all.at[z, T:H], csem.at[1])
            else:
                arrive("ctx%d" % (t - 1), S + g)
            cols = (slice(0, K // 2), slice(K // 2, K)) if t == 3 else (slice(0, K), slice(0, K))
            up_piece, down_piece = ctx_all.at[zi(-t), span, cols[0]], ctx_all.at[zi(t), span, cols[1]]
            send("ctx%d" % t, S + g, [(up_piece, up_piece, zp(1)), (down_piece, down_piece, zp(-1))])
        return step

    def scatter(name, s, product, piece, landing):
        k = part(s)
        piece[:, :, k, :] = product.astype(jnp.bfloat16).reshape(2, 4, T, 2 * F)
        send(name, s, [(piece.at[:, low(yi(d)), k, :], landing.at[d - 1, :, k, :], yp(d)) for d in (1, 3, 2)])

    def scattered(name, s, piece, landing):
        arrive(name, s)
        k = part(s)
        total = piece[:, low(y), k, :].astype(jnp.float32)
        for d in range(3):
            total = total + landing[d, :, k, :].astype(jnp.float32)
        return total.reshape(2 * T, 2 * F)

    def project(s):
        if s == 0:
            arrive("spread", 0)
        else:
            arrive("ctx3", S + [s in members for members in GROUPS].index(True))
        ready("proj")
        product = jnp.dot(ctx_all[:, part(s), :].reshape(NZ * T, K), wproj[...], preferred_element_type=jnp.float32)
        scatter("project", s, product, att, rs)

    def mix(s):
        total = scattered("project", s, att, rs)
        k = part(s)
        if s == 0:
            landed(resb, csem.at[2])
            vec_swap[0].wait_recv()
        row_sum, row_square = jnp.zeros((2 * T, 128), jnp.float32), jnp.zeros((2 * T, 128), jnp.float32)
        for h in range(2):
            value = resb[h, :, k, :].reshape(2 * T, F).astype(jnp.float32) + total[:, h * F:(h + 1) * F] + vec[h, 0:1, :]
            mixed[h, s] = value
            for i in range(0, F, 128):
                row_sum = row_sum + value[:, i:i + 128]
                row_square = row_square + value[:, i:i + 128] * value[:, i:i + 128]
        pad = jnp.zeros((64 - 2 * T, 128), jnp.float32)
        by_lane = jnp.concatenate([row_sum, pad, row_square, pad], axis=0).T
        st[s, z] = jnp.sum(by_lane, axis=0, keepdims=True)
        send("mix", s, [(st.at[s, z], st.at[s, z], zp(d)) for d in (4, 3, 5, 2, 6, 1, 7)])

    def norm(s):
        arrive("mix", s)
        k = part(s)
        total = jnp.broadcast_to(jnp.sum(st[s], axis=0), (128, 128)).T
        mean = total[0:2 * T, 0:1] / D
        var = total[64:64 + 2 * T, 0:1] / D - mean * mean
        scale = lax.rsqrt(var + 1e-05)
        for h in range(2):
            normed = (mixed[h, s] - mean) * scale * vec[h, 1:2, :] + vec[h, 2:3, :]
            nrm[:, low(y), k, h * F:(h + 1) * F] = normed.astype(jnp.bfloat16).reshape(2, T, F)
        piece = nrm.at[:, low(y), k, :]
        send("norm", s, [(piece, piece, yp(d)) for d in (1, 3, 2)])


    def columns(s, u):
        start, stop = PARTS[s][u]
        middle = (start + stop) // 2
        return slice(start, stop), (slice(start, middle), slice(middle, stop))

    def up(s, u):
        if u == 0:
            arrive("norm", s)
        ready("up", (s, u) == (0, 0))
        k, (cols, sides) = part(s), columns(s, u)
        product = jnp.dot(nrm[:, :, k, :].reshape(NZ * T, 2 * F), wup[:, cols], preferred_element_type=jnp.float32)
        prep[:, k, cols] = product.astype(jnp.bfloat16).reshape(NZ, T, cols.stop - cols.start)
        send(("up", u), s, [
            (prep.at[zi(4), k, sides[0]], zr.at[0, 0, k, sides[0]], zp(1)),
            (prep.at[zi(4), k, sides[1]], zr.at[1, 0, k, sides[1]], zp(-1)),
        ])

    def passing(t):
        def step(s, u):
            arrive(("up" if t == 1 else "pass%d" % (t - 1), u), s)
            k, (cols, sides), moves = part(s), columns(s, u), []
            for way, sign in ((0, 1), (1, -1)):
                at = zi(sign * (4 - t))
                came = cols if t > 1 else sides[way]
                prep[at, k, came] = (
                    prep[at, k, came].astype(jnp.float32) + zr[way, t - 1, k, came].astype(jnp.float32)
                ).astype(jnp.bfloat16)
                moves.append((prep.at[at, k, cols], zr.at[way, t, k, cols], zp(sign)))
            send(("pass%d" % t, u), s, moves)
        return step

    def gelu(s, u):
        arrive(("pass3", u), s)
        if (s, u) == (0, 0):
            for copy in uvec_gather:
                copy.wait_recv()
        k, (cols, _) = part(s), columns(s, u)
        for i in range(cols.start, cols.stop, F):
            at = slice(i, i + F)
            total = prep[z, k, at].astype(jnp.float32) + zr[0, 3, k, at].astype(jnp.float32)
            unit = i % (2 * F)
            total = total + zr[1, 3, k, at].astype(jnp.float32) + uvec[i // (2 * F), 0:1, unit:unit + F]
            hid[z, k, at] = jax.nn.gelu(total, approximate=True).astype(jnp.bfloat16)
        piece = hid.at[z, k, cols]
        send(("gelu", u), s, [(piece, piece, zp(1)), (piece, piece, zp(-1))])

    def handing(t):
        def step(s, u):
            arrive(("gelu" if t == 1 else "hand%d" % (t - 1), u), s)
            cols, sides = columns(s, u)
            ways = sides if t == 3 else (cols, cols)
            up_piece, down_piece = hid.at[zi(-t), part(s), ways[0]], hid.at[zi(t), part(s), ways[1]]
            send(("hand%d" % t, u), s, [(up_piece, up_piece, zp(1)), (down_piece, down_piece, zp(-1))])
        return step

    def down(s):
        for u in range(len(PARTS[s])):
            arrive(("hand3", u), s)
        ready("down")
        product = jnp.dot(hid[:, part(s), :].reshape(NZ * T, U), wdown[...], preferred_element_type=jnp.float32)
        scatter("down", s, product, outp, os)

    def finish(s):
        total = scattered("down", s, outp, os)
        for h in range(2):
            value = mixed[h, s] + total[:, h * F:(h + 1) * F] + vec[h, 3:4, :]
            obuf[h, s] = value.astype(jnp.bfloat16)
        for h in range(2):
            for k in range(2):
                give(obuf.at[h, s, k * T:(k + 1) * T], out.at[rows(128 * c + 64 * (x % 2) + s * T, T)],
                     gsem.at[12 + s * 4 + h * 2 + k], csem.at[3], h, (x // 2 + y) % 2 + 2 * k)

    stages = {("spread", "project", "mix", "norm", "down", "finish")[i]: f
              for i, f in enumerate((spread, project, mix, norm, down, finish))}
    for t in range(4):
        stages["ctx%d" % t] = ring(t)
    by_part = dict(up=up, gelu=gelu)
    for t in range(1, 4):
        by_part["pass%d" % t], by_part["hand%d" % t] = passing(t), handing(t)
    for name, s, u in issue_order()[0]:
        if name in by_part:
            by_part[name](s, u)
        elif name == "relay_proj":
            relay("proj")
            give_residual()
            gather("up", 10)
        elif name == "relay_up":
            relay("up")
        elif name == "relay_down":
            relay("down")
        elif name.startswith("share_"):
            share(name[6:])
            if name == "share_up":
                gather("down", 20)
        else:
            stages[name](s)
        clear(60)
    clear(0)
    landed(out, csem.at[3])


def layer(context, residual_in, proj_weight, proj_bias, norm_gain, norm_shift, up_weight, up_bias, down_weight, down_bias):
    bf16, f32 = jnp.bfloat16, jnp.float32
    hbm = pl.BlockSpec(memory_space=pl.ANY)
    dma = pltpu.SemaphoreType.DMA
    return pl.pallas_call(
        kernel,
        out_shape=jax.ShapeDtypeStruct((256, F), bf16),
        in_specs=[hbm] * 10,
        out_specs=hbm,
        scratch_shapes=[
            pltpu.VMEM((NZ, H, K), bf16),
            pltpu.VMEM((K, 2 * F), bf16),
            pltpu.VMEM((2 * F, U), bf16),
            pltpu.VMEM((U, 2 * F), bf16),
            pltpu.VMEM((2, 2, H, F), bf16),
            *[pltpu.VMEM((F,), bf16)] * 4,
            pltpu.VMEM((2 * F,), bf16),
            pltpu.VMEM((2, 8, F), f32),
            pltpu.VMEM((NX, 8, 2 * F), f32),
            pltpu.VMEM((2, 4, H, 2 * F), bf16),
            pltpu.VMEM((3, 2, H, 2 * F), bf16),
            pltpu.VMEM((2, S, 2 * T, F), f32),
            pltpu.VMEM((S, NZ, 1, 128), f32),
            pltpu.VMEM((2, 4, H, 2 * F), bf16),
            pltpu.VMEM((NZ, H, U), bf16),
            pltpu.VMEM((2, 4, H, U), bf16),
            pltpu.VMEM((NZ, H, U), bf16),
            pltpu.VMEM((2, 4, H, 2 * F), bf16),
            pltpu.VMEM((3, 2, H, 2 * F), bf16),
            pltpu.VMEM((2, S, 2 * T, F), bf16),
            dma((S + len(GROUPS), 56)),
            dma((S + len(GROUPS), 56)),
            dma((34,)),
            dma((34,)),
            dma((4,)),
            dma((12 + 4 * S,)),
            dma((8,)),
        ],
        compiler_params=pltpu.CompilerParams(
            collective_id=0, has_side_effects=True, vmem_limit_bytes=56 * 2**20
        ),
        name="layer",
    )(context, residual_in, proj_weight, proj_bias, norm_gain, norm_shift, up_weight, up_bias, down_weight, down_bias)


def solution(mesh):
    return jax.shard_map(
        layer,
        mesh=mesh,
        in_specs=(
            P("row", "col"),
            P("col", "row"),
            P("col", "row"),
            P("row"),
            P("row"),
            P("row"),
            P("row", "col"),
            P("col"),
            P("col", "row"),
            P("row"),
        ),
        out_specs=P("col", "row"),
        check_vma=False,
    )
```

```python
import jax
import jax.numpy as jnp
from jax import lax
from jax.experimental import pallas as pl
from jax.experimental.pallas import tpu as pltpu
from jax.sharding import PartitionSpec as P

D = 6144
F = 384
K = 4 * F
U = 8 * F
H = 64
S = 4
T = H // S
GROUPS = ((1,), (2, 3))
NZ, NX, NY = 8, 4, 4
MESH = pl.DeviceIdType.MESH

PARTS = (((0, 3 * U // 4), (3 * U // 4, U)),) * 2 + (((0, U),),) * (S - 2)
RATE = 50000.0
Z_STEPS = ("up", "pass1", "pass2", "pass3", "gelu", "hand1", "hand2", "hand3")
Z_WORK = dict(up=0.9, pass1=0.25, pass2=0.25, pass3=0.25, gelu=0.5)


def issue_order():
    nodes = {
        ("relay_proj", 0, 0): ((), 16.5, 0.0, 4, "x", 0, 0.0),
        ("share_proj", 0, 0): ((("relay_proj", 0, 0),), 20.0, 0.0, 2, "x", 0, 0.0),
        ("relay_up", 0, 0): ((("share_proj", 0, 0),), 34.5, 0.0, 4, "x", 0, 0.0),
        ("share_up", 0, 0): ((("relay_up", 0, 0),), 41.0, 0.0, 2, "x", 0, 0.0),
        ("relay_down", 0, 0): ((("share_up", 0, 0),), 62.0, 0.0, 4, "x", 0, 0.0),
        ("share_down", 0, 0): ((("relay_down", 0, 0),), 75.0, 0.0, 2, "x", 0, 0.0),
        ("spread", 0, 0): ((), 14.0, 0.0, 7, "z", 393216, 4.3),
    }
    arrived = {0: ("spread", 0, 0)}
    for s in range(S):
        if s > 0:
            g = [s in members for members in GROUPS].index(True)
            arrived[s] = ("ctx3", g, 0)
        nodes["project", s, 0] = ((arrived[s],), 25.0, 0.6, 3, "y", 98304, 2.7)
        nodes["mix", s, 0] = ((("project", s, 0),), 0.0, 0.6, 7, "z", 0, 4.3)
        nodes["norm", s, 0] = ((("mix", s, 0),), 0.0, 0.5, 3, "y", 98304, 2.7)
        for u, (first_unit, last_unit) in enumerate(PARTS[s]):
            share = (last_unit - first_unit) / U
            before = ("norm", s, 0)
            for name in Z_STEPS:
                size = 98304 * share * (0.5 if name in ("up", "hand3") else 1)
                nodes[name, s, u] = ((before,), 54.0 if name == "up" and u == len(PARTS[s]) - 1 else 0.0, Z_WORK.get(name, 0.0) * share, 2, "z", size, 2.8)
                before = (name, s, u)
        nodes["down", s, 0] = (tuple(("hand3", s, u) for u in range(len(PARTS[s]))), 0.0, 0.9, 3, "y", 98304, 2.7)
        nodes["finish", s, 0] = ((("down", s, 0),), 0.0, 0.4, 4, "x", 49152, 2.7)
    for g, members in enumerate(GROUPS):
        for t in range(4):
            size = 49152 * len(members) * (0.5 if t == 3 else 1)
            nodes["ctx%d" % t, g, 0] = (((("ctx%d" % (t - 1), g, 0),) if t else ()), 20.5 if t == 0 else 0.0, 0.0, 2, "z", size, 2.8)
    urgency = {node: (node[0].startswith("ctx"), node[1], node[2]) for node in nodes}
    free, now, order, done = {"z": 0.0, "y": 0.0, "x": 0.0}, 0.0, [], {}
    while len(order) < len(nodes):
        due = {
            node: max([start] + [done[n] for n in after])
            for node, (after, start, *_) in nodes.items()
            if node not in done and all(n in done for n in after)
        }
        first = min(due.values())
        node = min((n for n in due if due[n] <= max(now, first)), key=lambda n: (urgency[n], n))
        _, _, work, copies, link, size, latency = nodes[node]
        now = max(now, due[node]) + work + 0.06 * copies
        free[link] = max(free[link], now) + size / RATE
        done[node] = free[link] + latency
        order.append(node)
    return order, max(done.values())


def kernel(ctx, res, wp, pb, ng, ns, wu, ub, wd, db, out,
           ctx_all, wproj, wup, wdown, resb, vin0, vin1, vin2, vin3, uin, vec, uvec, att, rs, mixed, st, nrm, prep, zr, hid,
           outp, os, obuf, ssem, rsem, wssem, wrsem, csem, gsem, lsem):
    r, q = lax.axis_index("row"), lax.axis_index("col")
    z, c = r // 2, r % 2
    x, y = q // 4, q % 4
    sib = (z * 2 + 1 - c, q)

    def zi(d):
        return (z + d + NZ) % NZ

    def yi(d):
        return (y + d) % NY

    def zp(d):
        return (zi(d) * 2 + c, q)

    def xp(d):
        return (r, ((x + d) % NX) * 4 + y)

    def yp(d):
        return (r, x * 4 + yi(d))

    def rows(start, size):
        return pl.ds(pl.multiple_of(start, 16), size)

    def lanes(start, size):
        return pl.ds(pl.multiple_of(start, 128), size)

    def local(src, dst, sem):
        copy = pltpu.make_async_copy(src, dst, sem)
        copy.start()
        return copy

    sends = []

    def remote(src, dst, send, recv, device):
        copy = pltpu.make_async_remote_copy(
            src_ref=src, dst_ref=dst, send_sem=send, recv_sem=recv, device_id=device, device_id_type=MESH
        )
        copy.start()
        sends.append((None, copy))
        return copy

    def give(src, dst, send, recv, to_core, to_x):
        here = (to_core == c) & (to_x == x)
        copy = pltpu.make_async_remote_copy(
            src_ref=src, dst_ref=dst, send_sem=send, recv_sem=recv, device_id=(z * 2 + to_core, to_x * 4 + y),
            device_id_type=MESH,
        )

        @pl.when(here)
        def _():
            pltpu.make_async_copy(src, dst, recv).start()

        @pl.when(jnp.logical_not(here))
        def _():
            copy.start()

        sends.append((here, copy))

    def clear(keep):
        while len(sends) > keep:
            here, copy = sends.pop(0)
            if here is None:
                copy.wait_send()
            else:
                pl.when(jnp.logical_not(here))(copy.wait_send)

    def landed(ref, sem):
        pltpu.make_async_copy(ref, ref, sem).wait()

    vin = (vin0, vin1, vin2, vin3)
    half = lanes(c * F, F)
    places = {
        "proj": lambda slot: wproj.at[slot * F:(slot + 1) * F, half],
        "up": lambda slot: wup.at[rows(c * F, F), slot * 2 * F:(slot + 1) * 2 * F],
        "down": lambda slot: wdown.at[slot * 2 * F:(slot + 1) * 2 * F, half],
    }
    blocks = {"proj": wp, "up": wu, "down": wd}
    vector_in = [local(v, vin[i], lsem.at[i]) for i, v in enumerate((pb, ng, ns, db))] + [local(ub, uin, lsem.at[4])]
    own = {name: local(blocks[name], places[name](0), lsem.at[5 + i]) for i, name in enumerate(blocks)}

    barrier = pltpu.get_barrier_semaphore()
    partners = [sib] + [zp(d) for d in range(1, NZ)] + [yp(d) for d in range(1, NY)]
    partners += [p for d in range(1, NX) for p in (xp(d), (sib[0], xp(d)[1]))]
    for p in partners:
        pl.semaphore_signal(barrier, inc=1, device_id=p, device_id_type=MESH)
    pl.semaphore_wait(barrier, len(partners))

    gathers = {}

    def swap(name, i, src, dst):
        return remote(src, dst, wssem.at[i], wrsem.at[i], sib)

    def halves(place):
        n = place.shape[0] // 2
        return place.at[0:n], place.at[n:2 * n]

    def gather(name, i):
        block, near = halves(blocks[name]), {}
        for first in (True, False):
            for j, d in ((0, 1), (1, 3)):
                k = j if first else 1 - j
                n = i + 2 * j + (0 if first else 1)
                near[j, first] = remote(block[k], halves(places[name](1 + j))[k], wssem.at[n], wrsem.at[n], xp(d))
        gathers[name] = (near, [swap(name, i + 4, blocks[name], places[name](0))], [], i)

    ctx_side = (c + z // 2) % 2

    def slot_at(at):
        d = (x - at + NX) % NX
        return jnp.where(d == 3, 1, jnp.where(d == 0, 0, d + 1))

    def give_context(g, low, size):
        for i in range(2):
            for core in range(2):
                give(ctx.at[rows(128 * core + 64 * i + low, size)], ctx_all.at[z, low:low + size, lanes(slot_at(2 * ctx_side + i) * F, F)],
                     gsem.at[g * 4 + i * 2 + core], csem.at[g], core, 2 * ctx_side + i)

    def give_residual():
        side = (x + y) % 2
        for i in range(2):
            for core in range(2):
                give(res.at[rows(128 * core + 64 * i, H)], resb.at[c, x // 2], gsem.at[8 + i * 2 + core], csem.at[2],
                     core, 2 * side + i)

    give_context(0, 0, T)
    gather("proj", 0)
    give_context(1, T, H - T)
    for copy in vector_in:
        copy.wait()
    for i in range(4):
        vec[c, i:i + 1, :] = vin[i][...].reshape(1, F).astype(jnp.float32)
    uvec[0, 0:1, :] = uin[...].reshape(1, 2 * F).astype(jnp.float32)
    vec_swap = [swap("vec", 30, vec.at[c], vec.at[c])]
    uvec_gather = [remote(uvec.at[0], uvec.at[{1: 1, 3: 2, 2: 3}[d]], wssem.at[30 + d], wrsem.at[30 + d], xp(d)) for d in (1, 3, 2)]

    def relay(name):
        near, far, relays, i = gathers[name]
        for j, to in ((0, 1), (1, 3)):
            near[j, True].wait_recv()
            piece, goal = halves(places[name](1 + j))[j], halves(places[name](3))[j]
            relays.append(remote(piece, goal, wssem.at[i + 5 + j], wrsem.at[i + 5 + j], xp(to)))

    def share(name):
        near, far, relays, i = gathers[name]
        for j in range(2):
            near[j, False].wait_recv()
            far.append(swap(name, i + 7 + j, places[name](1 + j), places[name](1 + j)))

    def ready(name, near_only=False):
        if name in own:
            own.pop(name).wait()
            for copy in gathers[name][1]:
                copy.wait_recv()
        if name in gathers and not near_only:
            near, far, relays, i = gathers.pop(name)
            for copy in relays:
                copy.wait_recv()
            swap(name, i + 9, places[name](3), places[name](3)).wait_recv()

    flights, slots = {}, {}

    def send(name, s, moves):
        copies = []
        for src, dst, device in moves:
            i = slots[s] = slots.get(s, -1) + 1
            copies.append(remote(src, dst, ssem.at[s, i], rsem.at[s, i], device))
        flights[name, s] = copies

    def arrive(name, s):
        for copy in flights.pop((name, s), ()):
            copy.wait_recv()

    def part(s):
        return slice(s * T, (s + 1) * T)

    def low(at):
        return 2 * ((x // 2 + at) % 2) + at // 2

    def spread(s):
        landed(ctx_all.at[z, 0:T], csem.at[0])
        piece = ctx_all.at[z, part(0), :]
        send("spread", 0, [(piece, piece, zp(d)) for d in (4, 3, 5, 2, 6, 1, 7)])

    def ring(t):
        def step(g):
            members = GROUPS[g]
            span = slice(members[0] * T, (members[-1] + 1) * T)
            if t == 0:
                if g == 0:
                    landed(ctx_all.at[z, T:H], csem.at[1])
            else:
                arrive("ctx%d" % (t - 1), S + g)
            cols = (slice(0, K // 2), slice(K // 2, K)) if t == 3 else (slice(0, K), slice(0, K))
            up_piece, down_piece = ctx_all.at[zi(-t), span, cols[0]], ctx_all.at[zi(t), span, cols[1]]
            send("ctx%d" % t, S + g, [(up_piece, up_piece, zp(1)), (down_piece, down_piece, zp(-1))])
        return step

    def scatter(name, s, product, piece, landing):
        k = part(s)
        piece[:, :, k, :] = product.astype(jnp.bfloat16).reshape(2, 4, T, 2 * F)
        send(name, s, [(piece.at[:, low(yi(d)), k, :], landing.at[d - 1, :, k, :], yp(d)) for d in (1, 3, 2)])

    def scattered(name, s, piece, landing):
        arrive(name, s)
        k = part(s)
        total = piece[:, low(y), k, :].astype(jnp.float32)
        for d in range(3):
            total = total + landing[d, :, k, :].astype(jnp.float32)
        return total.reshape(2 * T, 2 * F)

    def project(s):
        if s == 0:
            arrive("spread", 0)
        else:
            arrive("ctx3", S + [s in members for members in GROUPS].index(True))
        ready("proj")
        product = jnp.dot(ctx_all[:, part(s), :].reshape(NZ * T, K), wproj[...], preferred_element_type=jnp.float32)
        scatter("project", s, product, att, rs)

    def mix(s):
        total = scattered("project", s, att, rs)
        k = part(s)
        if s == 0:
            landed(resb, csem.at[2])
            vec_swap[0].wait_recv()
        row_sum, row_square = jnp.zeros((2 * T, 128), jnp.float32), jnp.zeros((2 * T, 128), jnp.float32)
        for h in range(2):
            value = resb[h, :, k, :].reshape(2 * T, F).astype(jnp.float32) + total[:, h * F:(h + 1) * F] + vec[h, 0:1, :]
            mixed[h, s] = value
            for i in range(0, F, 128):
                row_sum = row_sum + value[:, i:i + 128]
                row_square = row_square + value[:, i:i + 128] * value[:, i:i + 128]
        pad = jnp.zeros((64 - 2 * T, 128), jnp.float32)
        by_lane = jnp.concatenate([row_sum, pad, row_square, pad], axis=0).T
        st[s, z] = jnp.sum(by_lane, axis=0, keepdims=True)
        send("mix", s, [(st.at[s, z], st.at[s, z], zp(d)) for d in (4, 3, 5, 2, 6, 1, 7)])

    def norm(s):
        arrive("mix", s)
        k = part(s)
        total = jnp.broadcast_to(jnp.sum(st[s], axis=0), (128, 128)).T
        mean = total[0:2 * T, 0:1] / D
        var = total[64:64 + 2 * T, 0:1] / D - mean * mean
        scale = lax.rsqrt(var + 1e-05)
        for h in range(2):
            normed = (mixed[h, s] - mean) * scale * vec[h, 1:2, :] + vec[h, 2:3, :]
            nrm[:, low(y), k, h * F:(h + 1) * F] = normed.astype(jnp.bfloat16).reshape(2, T, F)
        piece = nrm.at[:, low(y), k, :]
        send("norm", s, [(piece, piece, yp(d)) for d in (1, 3, 2)])


    def columns(s, u):
        start, stop = PARTS[s][u]
        middle = (start + stop) // 2
        return slice(start, stop), (slice(start, middle), slice(middle, stop))

    def up(s, u):
        if u == 0:
            arrive("norm", s)
        ready("up", u < len(PARTS[s]) - 1)
        k, (cols, sides) = part(s), columns(s, u)
        product = jnp.dot(nrm[:, :, k, :].reshape(NZ * T, 2 * F), wup[:, cols], preferred_element_type=jnp.float32)
        prep[:, k, cols] = product.astype(jnp.bfloat16).reshape(NZ, T, cols.stop - cols.start)
        send(("up", u), s, [
            (prep.at[zi(4), k, sides[0]], zr.at[0, 0, k, sides[0]], zp(1)),
            (prep.at[zi(4), k, sides[1]], zr.at[1, 0, k, sides[1]], zp(-1)),
        ])

    def passing(t):
        def step(s, u):
            arrive(("up" if t == 1 else "pass%d" % (t - 1), u), s)
            k, (cols, sides), moves = part(s), columns(s, u), []
            for way, sign in ((0, 1), (1, -1)):
                at = zi(sign * (4 - t))
                came = cols if t > 1 else sides[way]
                prep[at, k, came] = (
                    prep[at, k, came].astype(jnp.float32) + zr[way, t - 1, k, came].astype(jnp.float32)
                ).astype(jnp.bfloat16)
                moves.append((prep.at[at, k, cols], zr.at[way, t, k, cols], zp(sign)))
            send(("pass%d" % t, u), s, moves)
        return step

    def gelu(s, u):
        arrive(("pass3", u), s)
        if (s, u) == (0, 0):
            for copy in uvec_gather:
                copy.wait_recv()
        k, (cols, _) = part(s), columns(s, u)
        for i in range(cols.start, cols.stop, F):
            at = slice(i, i + F)
            total = prep[z, k, at].astype(jnp.float32) + zr[0, 3, k, at].astype(jnp.float32)
            unit = i % (2 * F)
            total = total + zr[1, 3, k, at].astype(jnp.float32) + uvec[i // (2 * F), 0:1, unit:unit + F]
            hid[z, k, at] = jax.nn.gelu(total, approximate=True).astype(jnp.bfloat16)
        piece = hid.at[z, k, cols]
        send(("gelu", u), s, [(piece, piece, zp(1)), (piece, piece, zp(-1))])

    def handing(t):
        def step(s, u):
            arrive(("gelu" if t == 1 else "hand%d" % (t - 1), u), s)
            cols, sides = columns(s, u)
            ways = sides if t == 3 else (cols, cols)
            up_piece, down_piece = hid.at[zi(-t), part(s), ways[0]], hid.at[zi(t), part(s), ways[1]]
            send(("hand%d" % t, u), s, [(up_piece, up_piece, zp(1)), (down_piece, down_piece, zp(-1))])
        return step

    def down(s):
        for u in range(len(PARTS[s])):
            arrive(("hand3", u), s)
        ready("down")
        product = jnp.dot(hid[:, part(s), :].reshape(NZ * T, U), wdown[...], preferred_element_type=jnp.float32)
        scatter("down", s, product, outp, os)

    def finish(s):
        total = scattered("down", s, outp, os)
        for h in range(2):
            value = mixed[h, s] + total[:, h * F:(h + 1) * F] + vec[h, 3:4, :]
            obuf[h, s] = value.astype(jnp.bfloat16)
        for h in range(2):
            for k in range(2):
                give(obuf.at[h, s, k * T:(k + 1) * T], out.at[rows(128 * c + 64 * (x % 2) + s * T, T)],
                     gsem.at[12 + s * 4 + h * 2 + k], csem.at[3], h, (x // 2 + y) % 2 + 2 * k)

    stages = {("spread", "project", "mix", "norm", "down", "finish")[i]: f
              for i, f in enumerate((spread, project, mix, norm, down, finish))}
    for t in range(4):
        stages["ctx%d" % t] = ring(t)
    by_part = dict(up=up, gelu=gelu)
    for t in range(1, 4):
        by_part["pass%d" % t], by_part["hand%d" % t] = passing(t), handing(t)
    for name, s, u in issue_order()[0]:
        if name in by_part:
            by_part[name](s, u)
        elif name == "relay_proj":
            relay("proj")
            give_residual()
            gather("up", 10)
        elif name == "relay_up":
            relay("up")
        elif name == "relay_down":
            relay("down")
        elif name.startswith("share_"):
            share(name[6:])
            if name == "share_up":
                gather("down", 20)
        else:
            stages[name](s)
        clear(60)
    clear(0)
    landed(out, csem.at[3])


def layer(context, residual_in, proj_weight, proj_bias, norm_gain, norm_shift, up_weight, up_bias, down_weight, down_bias):
    bf16, f32 = jnp.bfloat16, jnp.float32
    hbm = pl.BlockSpec(memory_space=pl.ANY)
    dma = pltpu.SemaphoreType.DMA
    return pl.pallas_call(
        kernel,
        out_shape=jax.ShapeDtypeStruct((256, F), bf16),
        in_specs=[hbm] * 10,
        out_specs=hbm,
        scratch_shapes=[
            pltpu.VMEM((NZ, H, K), bf16),
            pltpu.VMEM((K, 2 * F), bf16),
            pltpu.VMEM((2 * F, U), bf16),
            pltpu.VMEM((U, 2 * F), bf16),
            pltpu.VMEM((2, 2, H, F), bf16),
            *[pltpu.VMEM((F,), bf16)] * 4,
            pltpu.VMEM((2 * F,), bf16),
            pltpu.VMEM((2, 8, F), f32),
            pltpu.VMEM((NX, 8, 2 * F), f32),
            pltpu.VMEM((2, 4, H, 2 * F), bf16),
            pltpu.VMEM((3, 2, H, 2 * F), bf16),
            pltpu.VMEM((2, S, 2 * T, F), f32),
            pltpu.VMEM((S, NZ, 1, 128), f32),
            pltpu.VMEM((2, 4, H, 2 * F), bf16),
            pltpu.VMEM((NZ, H, U), bf16),
            pltpu.VMEM((2, 4, H, U), bf16),
            pltpu.VMEM((NZ, H, U), bf16),
            pltpu.VMEM((2, 4, H, 2 * F), bf16),
            pltpu.VMEM((3, 2, H, 2 * F), bf16),
            pltpu.VMEM((2, S, 2 * T, F), bf16),
            dma((S + len(GROUPS), 56)),
            dma((S + len(GROUPS), 56)),
            dma((34,)),
            dma((34,)),
            dma((4,)),
            dma((12 + 4 * S,)),
            dma((8,)),
        ],
        compiler_params=pltpu.CompilerParams(
            collective_id=0, has_side_effects=True, vmem_limit_bytes=56 * 2**20
        ),
        name="layer",
    )(context, residual_in, proj_weight, proj_bias, norm_gain, norm_shift, up_weight, up_bias, down_weight, down_bias)


def solution(mesh):
    return jax.shard_map(
        layer,
        mesh=mesh,
        in_specs=(
            P("row", "col"),
            P("col", "row"),
            P("col", "row"),
            P("row"),
            P("row"),
            P("row"),
            P("row", "col"),
            P("col"),
            P("col", "row"),
            P("row"),
        ),
        out_specs=P("col", "row"),
        check_vma=False,
    )
```
